256 devices in a mesh: dp: 32 (over y, z), expert: 8 (over x, core).
Axes of the slice: x: 4, y: 4, z: 8, core: 2. Of those that a mesh axis runs over, the one named last changes fastest.
Arguments:
- tokens: bfloat16 [1024, 7168], P(('dp', 'expert')), may hold values from -6 to 6
- grad_out: bfloat16 [1024, 7168], P(('dp', 'expert')), may hold values from -6 to 6
- expert_ids: int32 [1024, 2], P(('dp', 'expert')), may hold values from 0 to 7, all different within a row; in each aligned block of 4 rows (0 to 3, 4 to 7, ...) at most 2 rows name the same one
- gate_values: float32 [1024, 2], P(('dp', 'expert')), may hold values from 0.1 to 1
- gate_master: float32 [8, 2048, 7168], P('expert', 'dp'), as said below
- gate_scale: float32 [8, 2048, 224], P('expert', 'dp'), as said below
- up_master: float32 [8, 2048, 7168], P('expert', 'dp'), as said below
- up_scale: float32 [8, 2048, 224], P('expert', 'dp'), as said below
- down_master: float32 [8, 2048, 7168], P('expert', 'dp'), as said below
- down_scale: float32 [8, 2048, 224], P('expert', 'dp'), as said below
Outputs:
- grad_tokens: bfloat16 [1024, 7168], P(('dp', 'expert'))
- grad_gate_master: float32 [8, 2048, 7168], P('expert', 'dp')
- grad_up_master: float32 [8, 2048, 7168], P('expert', 'dp')
- grad_down_master: float32 [8, 2048, 7168], P('expert', 'dp')
The draws below stay inside these ranges and needn't reach their ends.
Inputs may be any that keep to these rules, and one draw needn't show every extreme that they name: `expert_ids`: each token names two different experts; among the 4 tokens of one device (an aligned block of rows) no expert is named more than 2 times, a bound that some block reaches. gate_master divided by its group's gate_scale lies within 0.35 of an integer from -9 to 8 in every entry. `gate_scale`: positive scales. up_master divided by its group's up_scale lies within 0.35 of an integer from -9 to 8 in every entry. `up_scale`: positive scales. down_master divided by its group's down_scale lies within 0.35 of an integer from -9 to 8 in every entry. `down_scale`: positive scales.
All inputs are finite; a program needn't handle non-finite values.
Results may differ from the reference program's by a relative error of at most 0.022.
Values may be sent and summed in bfloat16 or wider, within the bound.
No kernel may reach another device: no remote copies, remote signals or barrier semaphores. Data moves between devices by JAX's collectives and lax.ppermute only.
A program may use at most 128 MiB of HBM per device.

```python
import math
import jax
import jax.numpy as jnp
import numpy as np
from jax import lax

D = 7168
FF = 2048
GROUP = 32
TOK_DEV = 4
CAP = 2
EXPERTS = 8
TOKENS = 1024
N_DP = 32
N_EXPERT = 8


def scale_table(key, salt, base, spread_log):
    sub_key = jax.random.fold_in(key, salt)
    spread = jax.random.uniform(sub_key, (EXPERTS, FF, D // GROUP), jnp.float32, -0.5, 0.5)
    return base * jnp.exp(spread_log * spread)


def master_table(key, scales):
    level_key, offset_key = jax.random.split(key)
    levels = jax.random.randint(level_key, (EXPERTS, FF, D), -9, 9).astype(jnp.float32)
    offsets = jax.random.uniform(offset_key, (EXPERTS, FF, D), jnp.float32, -0.35, 0.35)
    return (levels + offsets) * jnp.repeat(scales, GROUP, axis=2)


def spread_width():
    return math.log(4.0)


def draw_gate_scale(key, part):
    return scale_table(key, 101, 0.0023, spread_width())


def draw_gate_master(key, part):
    scales = scale_table(key, 101, 0.0023, spread_width())
    key = jax.random.fold_in(key, 1)
    return master_table(key, scales)


def draw_up_scale(key, part):
    return scale_table(key, 202, 0.0023, spread_width())


def draw_up_master(key, part):
    scales = scale_table(key, 202, 0.0023, spread_width())
    key = jax.random.fold_in(key, 2)
    return master_table(key, scales)


def draw_down_scale(key, part):
    return scale_table(key, 303, 0.0042, spread_width())


def draw_down_master(key, part):
    scales = scale_table(key, 303, 0.0042, spread_width())
    key = jax.random.fold_in(key, 3)
    return master_table(key, scales)


def block_levels(own_key, dims, shards, low, largest):
    factor_of = 1.0
    for position, blocks in shards:
        heights = jax.random.uniform(jax.random.fold_in(jax.random.fold_in(own_key, 6), position), (blocks,), jnp.float32, low / len(shards), largest / len(shards))
        factor_of = factor_of * jnp.repeat(jnp.exp(heights), dims[position] // blocks).reshape((-1,) + (1,) * (len(dims) - 1 - position))
    return factor_of


def assign_block(stream_key, own, number, rows, count, top, most, skew):
    order = jax.random.permutation(stream_key, count)
    crowded, ordinary = load_shares(count, rows * top, most, skew, True), load_shares(count, rows * top, most, skew, False)
    places = jnp.arange(count)

    def named(lengths, rotation):
        used = int((lengths > 0).sum())
        fixed = max(1, used // 4)
        moved = fixed + (places - fixed + rotation * (used - fixed)) % max(1, count - fixed)
        return jnp.zeros((count,), jnp.int32).at[order[jnp.where(places < fixed, places, moved)]].set(jnp.asarray(lengths, jnp.int32))

    lengths = jnp.where(number % 4 == 0, named(crowded, number // 4), named(ordinary, number - number // 4 - 1))
    mixed = jax.random.permutation(jax.random.fold_in(own, 3), count)
    giver, sink = mixed[0:count // 2 * 2:2], mixed[1:count // 2 * 2:2]
    margin = jnp.minimum(lengths[giver] - 1, most - lengths[sink]) // 2
    margin = jnp.where((giver == order[0]) | (sink == order[0]) | (lengths[sink] == 0), 0, jnp.maximum(margin, 0))
    moved = jax.random.randint(jax.random.fold_in(own, 4), (count // 2,), 0, 1 << 20) % (margin + 1)
    lengths = lengths.at[giver].add(-moved).at[sink].add(moved)
    members = jnp.searchsorted(jnp.cumsum(lengths), jnp.arange(rows * top), side="right").astype(jnp.int32)
    grid = members.reshape(top, rows).T
    grid = grid[jax.random.permutation(jax.random.fold_in(own, 1), rows)]
    rotation = jax.random.randint(jax.random.fold_in(own, 2), (rows, 1), 0, top)
    return jnp.take_along_axis(grid, (jnp.arange(top)[None, :] + rotation) % top, axis=1)


def load_shares(amount, total, most, slope, full):
    weights = [(1 << 20) // math.isqrt(standing ** slope) + 1 for standing in range(1, amount + 1)]
    largest = most if full else min(most, max(-(-total // amount), total * weights[0] // sum(weights)))
    least = 1 if total - largest >= amount - 1 else 0
    holding, spare = [largest] + [least] * (amount - 1), total - largest - least * (amount - 1)
    while spare > 0:
        candidates = [i for i in range(1, amount) if holding[i] < largest] or [i for i in range(1, amount) if holding[i] < most]
        whole, budget = sum([weights[i] for i in candidates]), spare
        for i in candidates:
            extra = min(most - holding[i], max(1, budget * weights[i] // whole), spare)
            holding[i] = holding[i] + extra
            spare = spare - extra
    return np.array(holding)


def centred(rng, extent, scale, limit, shards=(), kind=jnp.bfloat16):
    values = jax.random.normal(rng, extent, jnp.float32) * scale
    if len(shards) > 0:
        values = block_levels(rng, extent, shards, -0.22, 0.18) * values
    return jnp.clip(values, min=-limit, max=limit).astype(kind)


def setup_inputs(seed: int = 0) -> dict:
    seeds = jax.random.split(jax.random.key(seed), 11)
    tokens = centred(seeds[0], (TOKENS, D), 1.0, 6.0, ((0, 256),))
    grad_out = centred(seeds[1], (TOKENS, D), 1.0, 6.0, ((0, 256),))
    expert_ids_keys = jax.random.split(jax.random.fold_in(seeds[2], 1), TOKENS // TOK_DEV)
    expert_ids_turns = jax.random.permutation(jax.random.fold_in(seeds[2], 3), TOKENS // TOK_DEV)
    expert_ids = jax.vmap(lambda own, number: assign_block(jax.random.fold_in(seeds[2], 2), own, number, TOK_DEV, N_EXPERT, 2, CAP, 2))(expert_ids_keys, expert_ids_turns).reshape((TOKENS, 2))
    gate_values = jnp.clip(0.1 + 0.9 * jax.random.uniform(seeds[3], (TOKENS, 2), jnp.float32) ** block_levels(seeds[3], (TOKENS, 2), ((0, 256),), -0.2, 0.2), 0.1, 1.0)
    gate_master = draw_gate_master(jax.random.fold_in(seeds[10], 71), 0)
    gate_scale = draw_gate_scale(jax.random.fold_in(seeds[10], 71), 0)
    up_master = draw_up_master(jax.random.fold_in(seeds[10], 71), 0)
    up_scale = draw_up_scale(jax.random.fold_in(seeds[10], 71), 0)
    down_master = draw_down_master(jax.random.fold_in(seeds[10], 71), 0)
    down_scale = draw_down_scale(jax.random.fold_in(seeds[10], 71), 0)
    return {"tokens": tokens, "grad_out": grad_out, "expert_ids": expert_ids, "gate_values": gate_values, "gate_master": gate_master, "gate_scale": gate_scale, "up_master": up_master, "up_scale": up_scale, "down_master": down_master, "down_scale": down_scale}


def matmul_f32(left, right):
    return jnp.dot(left.astype(jnp.float32), right.astype(jnp.float32), preferred_element_type=jnp.float32)


def dequantize(master, scales):
    groups = scales.shape[-1]
    scaled = master.reshape(master.shape[0], groups, master.shape[1] // groups) / scales[:, :, None]
    levels = jnp.clip(jnp.floor(scaled + 0.5), -8.0, 7.0)
    weight = (levels * scales[:, :, None]).reshape(master.shape).astype(jnp.bfloat16)
    passed = jnp.where((scaled > -8.5) & (scaled < 7.5), 1.0, 0.0).astype(master.dtype).reshape(master.shape)
    return weight, passed


def expert_backward(rows_x, rows_dz, gate_w, up_w, down_w):
    gate_pre = matmul_f32(rows_x, gate_w.T)
    up_pre = matmul_f32(rows_x, up_w.T)
    sig_gate = jax.nn.sigmoid(gate_pre)
    silu_gate = gate_pre * sig_gate
    hidden = (silu_gate * up_pre).astype(jnp.bfloat16)
    delta_hidden = matmul_f32(rows_dz, down_w.T)
    delta_up = (delta_hidden * silu_gate).astype(jnp.bfloat16)
    delta_gate = (delta_hidden * up_pre * sig_gate * (1.0 + gate_pre * (1.0 - sig_gate))).astype(jnp.bfloat16)
    block_width = FF // N_DP

    def add_block(total, block):
        start = (block * block_width).astype(jnp.int32)
        gate_part = lax.dynamic_slice_in_dim(delta_gate, start, block_width, 1)
        up_part = lax.dynamic_slice_in_dim(delta_up, start, block_width, 1)
        gate_rows = lax.dynamic_slice_in_dim(gate_w, start, block_width, 0)
        up_rows = lax.dynamic_slice_in_dim(up_w, start, block_width, 0)
        partial_value = matmul_f32(gate_part, gate_rows) + matmul_f32(up_part, up_rows)
        partial_value = lax.optimization_barrier(partial_value.astype(jnp.bfloat16)).astype(jnp.float32)
        return total + partial_value, None

    zero_total = jnp.zeros((rows_x.shape[0], gate_w.shape[1]), jnp.float32)
    grad_x, unused = lax.scan(add_block, zero_total, jnp.arange(N_DP, dtype=jnp.int32))
    grad_gate = matmul_f32(delta_gate.T, rows_x)
    grad_up = matmul_f32(delta_up.T, rows_x)
    grad_down = matmul_f32(hidden.T, rows_dz)
    return grad_x, grad_gate, grad_up, grad_down


def reference(tokens, grad_out, expert_ids, gate_values, gate_master, gate_scale, up_master, up_scale, down_master, down_scale):
    row_limit = N_DP * N_EXPERT * CAP
    grad_rows = grad_out.astype(jnp.float32)

    def per_expert(inputs):
        expert, g_master, g_scale, u_master, u_scale, d_master, d_scale = inputs
        chosen = expert_ids == expert
        factor = jnp.sum(jnp.where(chosen, gate_values, jnp.zeros_like(gate_values)), axis=1)
        member = jnp.any(chosen, axis=1)
        picked = jnp.argsort(jnp.where(member, 0, 1).astype(jnp.int32), stable=True)[:row_limit].astype(jnp.int32)
        rows_x = tokens[picked]
        rows_dz = (factor[picked][:, None] * grad_rows[picked]).astype(jnp.bfloat16)
        gate_w, gate_keep = dequantize(g_master, g_scale)
        up_w, up_keep = dequantize(u_master, u_scale)
        down_w, down_keep = dequantize(d_master, d_scale)
        grad_x, grad_gate, grad_up, grad_down = expert_backward(rows_x, rows_dz, gate_w, up_w, down_w)
        return grad_x.astype(jnp.bfloat16), picked, grad_gate * gate_keep, grad_up * up_keep, grad_down * down_keep

    experts_all = jnp.arange(EXPERTS, dtype=jnp.int32)
    grad_x, picked, grad_gate, grad_up, grad_down = lax.map(per_expert, (experts_all, gate_master, gate_scale, up_master, up_scale, down_master, down_scale))
    total = jnp.zeros((TOKENS, D), jnp.float32)
    total = total.at[picked.reshape(-1)].add(grad_x.reshape(-1, D).astype(jnp.float32))
    return total.astype(jnp.bfloat16), grad_gate, grad_up, grad_down
```

```python
import jax
import jax.numpy as jnp
from jax import lax
from jax.sharding import PartitionSpec as P

NX = 4
X_GROUPS = [[0, 2, 4, 6], [1, 3, 5, 7]]
CORE_SWAP = [(i, i ^ 1) for i in range(8)]
BF = jnp.bfloat16
F32 = jnp.float32


def dequantize(master, scales):
    groups = scales.shape[-1]
    scaled = master.reshape(master.shape[0], groups, master.shape[1] // groups) / scales[:, :, None]
    levels = jnp.clip(jnp.floor(scaled + 0.5), -8.0, 7.0)
    weight = (levels * scales[:, :, None]).reshape(master.shape).astype(BF)
    passed = ((scaled > -8.5) & (scaled < 7.5)).reshape(master.shape)
    return (weight, passed)


def across_x(a):
    return lax.all_to_all(a, "expert", 0, 0, axis_index_groups=X_GROUPS, tiled=True)


def to_slices(a):
    return a.reshape(a.shape[0], NX, -1).transpose(1, 0, 2)


def from_slices(a):
    return a.transpose(1, 0, 2).reshape(a.shape[1], -1)


def nt(a, b):
    return lax.dot_general(a, b, (((1,), (1,)), ((), ())), preferred_element_type=F32)


def tn(a, b):
    return lax.dot_general(a, b, (((0,), (0,)), ((), ())), preferred_element_type=F32)


def per_device(
    tokens,
    grad_out,
    expert_ids,
    gate_values,
    gate_master,
    gate_scale,
    up_master,
    up_scale,
    down_master,
    down_scale,
):
    experts = lax.axis_size("expert")
    expert = lax.axis_index("expert")
    n_dp = lax.axis_size("dp")
    toks, width = tokens.shape
    hid = gate_master.shape[1]
    part = width // NX
    factor = jnp.sum(
        jnp.where(
            expert_ids[:, :, None] == jnp.arange(experts, dtype=jnp.int32), gate_values[:, :, None], 0.0
        ),
        axis=1,
    )
    f_hi = lax.reduce_precision(factor, 8, 7)
    f_mid = lax.reduce_precision(factor - f_hi, 8, 7)
    f_lo = factor - f_hi - f_mid
    f_cols = jnp.concatenate([f_hi, f_mid, f_lo], axis=1).astype(BF)
    f_cols = jnp.pad(f_cols, ((0, 0), (0, 128 - f_cols.shape[1])))
    payload = jnp.concatenate(
        [to_slices(tokens), to_slices(grad_out), jnp.broadcast_to(f_cols, (NX,) + f_cols.shape)], axis=2
    )
    mine = across_x(payload).reshape(NX * toks, -1)
    own = lax.all_gather(mine, "dp", axis=0, tiled=True)
    other = lax.ppermute(own, "expert", CORE_SWAP)
    halves = (own, other)
    half = own.shape[0]

    gate_w, gate_keep = dequantize(gate_master[0], gate_scale[0])
    up_w, up_keep = dequantize(up_master[0], up_scale[0])
    down_w, down_keep = dequantize(down_master[0], down_scale[0])
    w_all = across_x(to_slices(jnp.concatenate([gate_w, up_w, down_w], axis=0)))
    w_gu = w_all[:, : 2 * hid].reshape(NX * 2 * hid, part)
    w_d = w_all[:, 2 * hid :].reshape(NX * hid, part)

    pre_gu = jnp.concatenate([nt(w_gu, h[:, :part]) for h in halves], axis=1)
    pre_d = jnp.concatenate([nt(w_d, h[:, part : 2 * part]) for h in halves], axis=1)
    pre = jnp.concatenate(
        [pre_gu.reshape(NX, 2 * hid, 2 * half), pre_d.reshape(NX, hid, 2 * half)], axis=1
    ).astype(BF)
    pre = jnp.sum(across_x(pre).astype(F32), axis=0)
    picks = jnp.arange(128, dtype=jnp.int32)
    picks = ((picks % experts == expert) & (picks < 3 * experts)).astype(BF)
    weight = jnp.concatenate([nt(picks[None, :], h[:, 2 * part :]) for h in halves], axis=1)

    gate_pre, up_pre = pre[:hid], pre[hid : 2 * hid]
    delta_hidden = jnp.where(weight > 0.0, pre[2 * hid :] * weight, 0.0)
    sig_gate = jax.nn.sigmoid(gate_pre)
    silu_gate = gate_pre * sig_gate
    hidden = jnp.where(weight > 0.0, silu_gate * up_pre * weight, 0.0)
    delta_up = delta_hidden * silu_gate
    delta_gate = delta_hidden * up_pre * sig_gate * (1.0 + gate_pre * (1.0 - sig_gate))
    delta = jnp.concatenate([delta_gate, delta_up, hidden], axis=0).astype(BF)
    delta = lax.all_gather(delta, "expert", axis=0, axis_index_groups=X_GROUPS)
    d_gu = delta[:, : 2 * hid].reshape(NX * 2 * hid, 2 * half)
    d_h = delta[:, 2 * hid :].reshape(NX * hid, 2 * half)

    theirs = lax.ppermute(tn(d_gu[:, half:], w_gu).astype(BF), "expert", CORE_SWAP)
    grad_x = (tn(d_gu[:, :half], w_gu) + theirs.astype(F32)).astype(BF)
    grad_x = lax.all_to_all(grad_x.reshape(n_dp, NX * toks, part), "dp", 0, 0, tiled=True)
    grad_x = jnp.sum(grad_x.astype(F32), axis=0).astype(BF)
    grad_tokens = from_slices(across_x(grad_x.reshape(NX, toks, part)))

    g_gu = sum(
        jnp.dot(d_gu[:, i * half : (i + 1) * half], h[:, :part], preferred_element_type=F32)
        for i, h in enumerate(halves)
    )
    g_d = sum(
        jnp.dot(d_h[:, i * half : (i + 1) * half], h[:, part : 2 * part], preferred_element_type=F32)
        for i, h in enumerate(halves)
    )
    g_all = jnp.concatenate([g_gu.reshape(NX, 2 * hid, part), g_d.reshape(NX, hid, part)], axis=1)
    g_all = from_slices(across_x(g_all.astype(BF))).astype(F32)
    return (
        grad_tokens,
        jnp.where(gate_keep, g_all[:hid], 0.0)[None],
        jnp.where(up_keep, g_all[hid : 2 * hid], 0.0)[None],
        jnp.where(down_keep, g_all[2 * hid :], 0.0)[None],
    )


def solution(mesh):
    rows = P(("dp", "expert"), None)
    weights = P("expert", "dp", None)
    return jax.shard_map(
        per_device,
        mesh=mesh,
        in_specs=(rows,) * 4 + (weights,) * 6,
        out_specs=(rows,) + (weights,) * 3,
        check_vma=False,
    )
```

```python
import jax
import jax.numpy as jnp
from jax import lax
from jax.experimental import pallas as pl
from jax.experimental.pallas import tpu as pltpu
from jax.sharding import PartitionSpec as P

NX = 4
GROUP = 32
X_GROUPS = [[0, 2, 4, 6], [1, 3, 5, 7]]
CORE_SWAP = [(i, i ^ 1) for i in range(8)]
BF = jnp.bfloat16
F32 = jnp.float32
VMEM_LIMIT = 48 * 1024 * 1024


def shift_x(a, by):
    if by % NX == 0:
        return a
    return lax.ppermute(a, "expert", [(i, ((i // 2 + by) % NX) * 2 + i % 2) for i in range(2 * NX)])


def across_x(a):
    return lax.all_to_all(a, "expert", 0, 0, axis_index_groups=X_GROUPS, tiled=True)


def to_slices(a):
    return a.reshape(a.shape[0], NX, -1).transpose(1, 0, 2)


def from_slices(a):
    return a.transpose(1, 0, 2).reshape(a.shape[1], -1)


def nt(a, b):
    return lax.dot_general(a, b, (((1,), (1,)), ((), ())), preferred_element_type=F32)


def tn(a, b):
    return lax.dot_general(a, b, (((0,), (0,)), ((), ())), preferred_element_type=F32)


def mm(a, b):
    return jnp.dot(a, b, preferred_element_type=F32)


def three_terms(a):
    hi = a.astype(BF)
    rest = a - hi.astype(F32)
    mid = rest.astype(BF)
    return hi, mid, (rest - mid.astype(F32)).astype(BF)


def dequantize_kernel(x_ref, gm, um, dm, gs, us, ds, w0, w1, w2, w3, keep):
    hid, groups = gs.shape[1:]
    part = w0.shape[1]
    scales = three_terms(jnp.concatenate([gs[0], us[0], ds[0]], axis=0))
    group = lax.broadcasted_iota(jnp.int32, (groups, part), 0)
    lane_group = lax.broadcasted_iota(jnp.int32, (groups, part), 1) // GROUP
    for s, w in enumerate((w0, w1, w2, w3)):
        block = lax.rem(x_ref[0] + s, NX)
        col = pl.multiple_of(block * part, 128)
        spread = jnp.where(group == lane_group + block * (part // GROUP), 1.0, 0.0).astype(BF)
        scale = mm(scales[0], spread) + mm(scales[1], spread) + mm(scales[2], spread)
        for p, master in enumerate((gm, um, dm)):
            rows = slice(p * hid, (p + 1) * hid)
            unit = scale[rows]
            ratio = master[0, :, pl.ds(col, part)] / unit
            levels = jnp.clip(jnp.floor(ratio + 0.5), -8.0, 7.0)
            w[rows] = (levels * unit).astype(BF)
            keep[s, rows] = jnp.where((ratio > -8.5) & (ratio < 7.5), 1.0, 0.0).astype(BF)


def finish_kernel(x_ref, r0, r1, r2, r3, keep, og, ou, od):
    hid = og.shape[1]
    part = r0.shape[1]
    for s, r in enumerate((r0, r1, r2, r3)):
        col = pl.multiple_of(lax.rem(x_ref[0] + s, NX) * part, 128)
        for p, out in enumerate((og, ou, od)):
            rows = slice(p * hid, (p + 1) * hid)
            out[0, :, pl.ds(col, part)] = jnp.where(
                keep[s, rows].astype(F32) > 0.0, r[rows].astype(F32), 0.0
            )


def local_call(kernel, n_in, out_shape, cost):
    vmem = pl.BlockSpec(memory_space=pltpu.VMEM)
    return pl.pallas_call(
        kernel,
        out_shape=out_shape,
        in_specs=[pl.BlockSpec(memory_space=pltpu.SMEM)] + [vmem] * n_in,
        out_specs=[vmem] * len(out_shape),
        compiler_params=pltpu.CompilerParams(vmem_limit_bytes=VMEM_LIMIT),
        cost_estimate=pl.CostEstimate(flops=cost[0], bytes_accessed=cost[1], transcendentals=0),
    )


def per_device(
    tokens,
    grad_out,
    expert_ids,
    gate_values,
    gate_master,
    gate_scale,
    up_master,
    up_scale,
    down_master,
    down_scale,
):
    experts = lax.axis_size("expert")
    expert = lax.axis_index("expert")
    n_dp = lax.axis_size("dp")
    toks, width = tokens.shape
    hid = gate_master.shape[1]
    part = width // NX
    cap = toks // 2
    x_index = (expert // 2).reshape(1)

    named = expert_ids[:, :, None] == jnp.arange(experts, dtype=jnp.int32)
    factor = jnp.sum(jnp.where(named, gate_values[:, :, None], 0.0), axis=1)
    member = jnp.any(named, axis=1)
    rank = jnp.cumsum(member.astype(jnp.int32), axis=0) - 1
    f_hi = lax.reduce_precision(factor, 8, 7)
    f_mid = lax.reduce_precision(factor - f_hi, 8, 7)
    cols = [f_hi, f_mid, factor - f_hi - f_mid]
    cols += [jnp.where(member & (rank == slot), 1.0, 0.0) for slot in range(cap)]
    cols = jnp.concatenate(cols, axis=1).astype(BF)
    cols = jnp.pad(cols, ((0, 0), (0, 128 - cols.shape[1])))
    payload = jnp.concatenate(
        [to_slices(tokens), to_slices(grad_out), jnp.broadcast_to(cols, (NX,) + cols.shape)], axis=2
    )
    mine = across_x(payload).reshape(NX * toks, -1)
    own = lax.all_gather(mine, "dp", axis=0, tiled=True)
    other = lax.ppermute(own, "expert", CORE_SWAP)
    halves = (own, other)
    half = own.shape[0]
    blocks = half // toks

    sliced = jax.ShapeDtypeStruct((3 * hid, part), BF)
    *w_mine, keep = local_call(
        dequantize_kernel,
        6,
        [sliced] * NX + [jax.ShapeDtypeStruct((NX, 3 * hid, part), BF)],
        (30 * 3 * hid * width, 8 * 3 * hid * width),
    )(x_index, gate_master, up_master, down_master, gate_scale, up_scale, down_scale)
    w = [shift_x(a, s) for s, a in enumerate(w_mine)]
    w_gu = jnp.concatenate([a[: 2 * hid] for a in w], axis=0)
    w_d = jnp.concatenate([a[2 * hid :] for a in w], axis=0)

    pick = jnp.arange(128, dtype=jnp.int32)[:, None]
    owner = (jnp.arange(NX, dtype=jnp.int32)[None, :] * (experts - 2) + expert) % experts
    same_block = (
        jnp.arange(half, dtype=jnp.int32)[:, None] // toks == jnp.arange(blocks, dtype=jnp.int32)[None, :]
    )
    place = []
    for h in halves:
        slots = [
            mm(h[:, 2 * part :], (pick == owner + (3 + slot) * experts).astype(BF)) for slot in range(cap)
        ]
        place.append(
            [
                jnp.concatenate(
                    [jnp.where(same_block & (col[:, s : s + 1] > 0.5), 1.0, 0.0).astype(BF) for col in slots],
                    axis=1,
                )
                for s in range(NX)
            ]
        )
    pick_own = (pick % experts == expert) & (pick < 3 * experts)
    weight = jnp.concatenate(
        [
            jnp.sum(mm(h[:, 2 * part :], pick_own.astype(BF)) * place[i][0].astype(F32), axis=0)[None]
            for i, h in enumerate(halves)
        ],
        axis=1,
    )

    pre_gu = [nt(w_gu, h[:, :part]).astype(BF) for h in halves]
    pre_d = [nt(w_d, h[:, part : 2 * part]).astype(BF) for h in halves]
    pre = []
    for s in range(NX):
        packed = [
            mm(
                jnp.concatenate(
                    [pre_gu[i][s * 2 * hid : (s + 1) * 2 * hid], pre_d[i][s * hid : (s + 1) * hid]], axis=0
                ),
                place[i][s],
            )
            for i in range(2)
        ]
        pre.append(shift_x(jnp.concatenate(packed, axis=1).astype(BF), -s))
    pre = sum(a.astype(F32) for a in pre)

    gate_pre, up_pre = pre[:hid], pre[hid : 2 * hid]
    delta_hidden = jnp.where(weight > 0.0, pre[2 * hid :] * weight, 0.0)
    sig_gate = jax.nn.sigmoid(gate_pre)
    silu_gate = gate_pre * sig_gate
    hidden = jnp.where(weight > 0.0, silu_gate * up_pre * weight, 0.0)
    delta_up = delta_hidden * silu_gate
    delta_gate = delta_hidden * up_pre * sig_gate * (1.0 + gate_pre * (1.0 - sig_gate))
    delta = jnp.concatenate([delta_gate, delta_up, hidden], axis=0).astype(BF)
    delta = [shift_x(delta, s) for s in range(NX)]
    spread = [
        [
            nt(d[:, i * cap * blocks : (i + 1) * cap * blocks], place[i][s]).astype(BF)
            for s, d in enumerate(delta)
        ]
        for i in range(2)
    ]
    d_gu = [jnp.concatenate([d[: 2 * hid] for d in spread[i]], axis=0) for i in range(2)]
    d_h = [jnp.concatenate([d[2 * hid :] for d in spread[i]], axis=0) for i in range(2)]

    theirs = lax.ppermute(tn(d_gu[1], w_gu).astype(BF), "expert", CORE_SWAP)
    grad_x = (tn(d_gu[0], w_gu) + theirs.astype(F32)).astype(BF)
    grad_x = lax.all_to_all(grad_x.reshape(n_dp, NX * toks, part), "dp", 0, 0, tiled=True)
    grad_x = jnp.sum(grad_x.astype(F32), axis=0).astype(BF)
    grad_tokens = from_slices(across_x(grad_x.reshape(NX, toks, part)))

    g_gu = sum(mm(d_gu[i], h[:, :part]) for i, h in enumerate(halves)).astype(BF)
    g_d = sum(mm(d_h[i], h[:, part : 2 * part]) for i, h in enumerate(halves)).astype(BF)
    g_all = [
        shift_x(
            jnp.concatenate(
                [g_gu[s * 2 * hid : (s + 1) * 2 * hid], g_d[s * hid : (s + 1) * hid]], axis=0
            ),
            -s,
        )
        for s in range(NX)
    ]
    grads = local_call(
        finish_kernel,
        NX + 1,
        [jax.ShapeDtypeStruct((1, hid, width), F32)] * 3,
        (3 * 3 * hid * width, 8 * 3 * hid * width),
    )(x_index, *g_all, keep)
    return (grad_tokens, *grads)


def solution(mesh):
    rows = P(("dp", "expert"), None)
    weights = P("expert", "dp", None)
    return jax.shard_map(
        per_device,
        mesh=mesh,
        in_specs=(rows,) * 4 + (weights,) * 6,
        out_specs=(rows,) + (weights,) * 3,
        check_vma=False,
    )
```

```python
import jax
import jax.numpy as jnp
from jax import lax
from jax.experimental import pallas as pl
from jax.experimental.pallas import tpu as pltpu
from jax.sharding import PartitionSpec as P

NX, NY, NZ = 4, 4, 8
GROUP = 32
X_GROUPS = [[0, 2, 4, 6], [1, 3, 5, 7]]
CORE_SWAP = [(i, i ^ 1) for i in range(8)]
BF = jnp.bfloat16
F32 = jnp.float32
VMEM_LIMIT = 60 * 1024 * 1024


def shift_x(a, by):
    if by % NX == 0:
        return a
    return lax.ppermute(a, "expert", [(i, ((i // 2 + by) % NX) * 2 + i % 2) for i in range(2 * NX)])


def shift_y(a, by):
    if by == 0:
        return a
    return lax.ppermute(a, "dp", [(i, ((i // NZ + by) % NY) * NZ + i % NZ) for i in range(NY * NZ)])


def shift_z(a, by):
    if by == 0:
        return a
    return lax.ppermute(a, "dp", [(i, (i // NZ) * NZ + (i % NZ + by) % NZ) for i in range(NY * NZ)])


def gather_y(a):
    return jnp.concatenate([a] + [shift_y(a, -k) for k in range(1, NY)], axis=0)


def gather_z(a, early, late):
    after, before = [a], [a]
    for step in range(NZ // 2 - 1):
        if step == 2:
            (after[-1], before[-1]), early = lax.optimization_barrier(((after[-1], before[-1]), early))
        after.append(shift_z(after[-1], -1))
        before.append(shift_z(before[-1], 1))
    last, late = lax.optimization_barrier(((after[-1], before[-1]), late))
    cut = a.shape[0] // 2
    far = jnp.concatenate([shift_z(last[0][:cut], -1), shift_z(last[1][cut:], 1)], axis=0)
    return jnp.concatenate(after + [far] + before[:0:-1], axis=0), early, late


def in_order(a, z, y):
    a = lax.dynamic_slice_in_dim(jnp.concatenate([a, a], axis=0), NZ - z, NZ, 0)
    a = lax.dynamic_slice_in_dim(jnp.concatenate([a, a], axis=1), NY - y, NY, 1)
    return a.transpose(1, 0, 2, 3)


def placing(at, slots):
    return jnp.concatenate([jnp.where(at & (c > 0.5), 1.0, 0.0).astype(BF) for c in slots], axis=1)


def total(terms):
    return jnp.sum(terms.astype(F32), axis=0).astype(BF)


def across_x(a):
    return lax.all_to_all(a, "expert", 0, 0, axis_index_groups=X_GROUPS, tiled=True)


def to_slices(a):
    return a.reshape(a.shape[0], NX, -1).transpose(1, 0, 2)


def from_slices(a):
    return a.transpose(1, 0, 2).reshape(a.shape[1], -1)


def nt(a, b):
    return lax.dot_general(a, b, (((1,), (1,)), ((), ())), preferred_element_type=F32)


def tn(a, b):
    return lax.dot_general(a, b, (((0,), (0,)), ((), ())), preferred_element_type=F32)


def mm(a, b):
    return jnp.dot(a, b, preferred_element_type=F32)


def three_terms(a):
    hi = a.astype(BF)
    rest = a - hi.astype(F32)
    mid = rest.astype(BF)
    return hi, mid, (rest - mid.astype(F32)).astype(BF)


def dequantize_kernel(gm, um, dm, gs, us, ds, w, keep):
    hid, groups = gs.shape[1:]
    part = w.shape[2]
    scales = three_terms(jnp.concatenate([gs[0], us[0], ds[0]], axis=0))
    group = lax.broadcasted_iota(jnp.int32, (groups, part), 0)
    lane_group = lax.broadcasted_iota(jnp.int32, (groups, part), 1) // GROUP
    spread = jnp.where(group == lane_group + pl.program_id(0) * (part // GROUP), 1.0, 0.0).astype(BF)
    scale = mm(scales[0], spread) + mm(scales[1], spread) + mm(scales[2], spread)
    for p, master in enumerate((gm, um, dm)):
        rows = slice(p * hid, (p + 1) * hid)
        unit = scale[rows]
        ratio = master[0] / unit
        levels = jnp.clip(jnp.floor(ratio + 0.5), -8.0, 7.0)
        w[0, rows] = (levels * unit).astype(BF)
        keep[0, rows] = jnp.where((ratio > -8.5) & (ratio < 7.5), 1.0, 0.0).astype(BF)


def dequantize(masters, scales):
    _, hid, width = masters[0].shape
    part = width // NX
    out = pl.BlockSpec((1, 3 * hid, part), lambda i: (i, 0, 0))
    return pl.pallas_call(
        dequantize_kernel,
        grid=(NX,),
        out_shape=[jax.ShapeDtypeStruct((NX, 3 * hid, part), BF)] * 2,
        in_specs=[pl.BlockSpec((1, hid, part), lambda i: (0, 0, i))] * 3
        + [pl.BlockSpec(scales[0].shape, lambda i: (0, 0, 0))] * 3,
        out_specs=[out] * 2,
        compiler_params=pltpu.CompilerParams(vmem_limit_bytes=VMEM_LIMIT),
        cost_estimate=pl.CostEstimate(
            flops=30 * 3 * hid * width, bytes_accessed=8 * 3 * hid * width, transcendentals=0
        ),
    )(*masters, *scales)


def finish_kernel(x_ref, r0, r1, r2, r3, keep, og, ou, od):
    hid = og.shape[1]
    part = r0.shape[1]
    for s, r in enumerate((r0, r1, r2, r3)):
        block = lax.rem(x_ref[0] + s, NX)
        col = pl.multiple_of(block * part, 128)
        for p, out in enumerate((og, ou, od)):
            rows = slice(p * hid, (p + 1) * hid)
            out[0, :, pl.ds(col, part)] = jnp.where(
                keep[block, rows].astype(F32) > 0.0, r[rows].astype(F32), 0.0
            )


def local_call(kernel, n_in, out_shape, cost):
    vmem = pl.BlockSpec(memory_space=pltpu.VMEM)
    return pl.pallas_call(
        kernel,
        out_shape=out_shape,
        in_specs=[pl.BlockSpec(memory_space=pltpu.SMEM)] + [vmem] * n_in,
        out_specs=[vmem] * len(out_shape),
        compiler_params=pltpu.CompilerParams(vmem_limit_bytes=VMEM_LIMIT),
        cost_estimate=pl.CostEstimate(flops=cost[0], bytes_accessed=cost[1], transcendentals=0),
    )


def per_device(
    tokens,
    grad_out,
    expert_ids,
    gate_values,
    gate_master,
    gate_scale,
    up_master,
    up_scale,
    down_master,
    down_scale,
):
    experts = lax.axis_size("expert")
    expert = lax.axis_index("expert")
    toks, width = tokens.shape
    hid = gate_master.shape[1]
    part = width // NX
    cap = toks // 2
    x_index = (expert // 2).reshape(1)

    named = expert_ids[:, :, None] == jnp.arange(experts, dtype=jnp.int32)
    factor = jnp.sum(jnp.where(named, gate_values[:, :, None], 0.0), axis=1)
    member = jnp.any(named, axis=1)
    rank = jnp.cumsum(member.astype(jnp.int32), axis=0) - 1
    f_hi = lax.reduce_precision(factor, 8, 7)
    f_mid = lax.reduce_precision(factor - f_hi, 8, 7)
    cols = [f_hi, f_mid, factor - f_hi - f_mid]
    cols += [jnp.where(member & (rank == slot), 1.0, 0.0) for slot in range(cap)]
    cols = jnp.concatenate(cols, axis=1).astype(BF)
    cols = jnp.pad(cols, ((0, 0), (0, 128 - cols.shape[1])))
    payload = jnp.concatenate(
        [to_slices(tokens), jnp.broadcast_to(cols, (NX,) + cols.shape), to_slices(grad_out)], axis=2
    )
    mine = across_x(payload).reshape(NX * toks, -1)
    w_mine, keep = dequantize(
        (gate_master, up_master, down_master), (gate_scale, up_scale, down_scale)
    )
    w_mine = [
        lax.dynamic_index_in_dim(w_mine, (expert // 2 + s) % NX, 0, keepdims=False) for s in range(NX)
    ]
    own, w_mine = lax.optimization_barrier((gather_y(mine), w_mine))
    w = [shift_x(a, s) if s != 2 else a for s, a in enumerate(w_mine)]
    w = lax.optimization_barrier(w)
    own, (w[1], w[3]), w[2] = gather_z(own, (w[1], w[3]), shift_x(w[2], 2))
    halves = (own, lax.ppermute(own, "expert", CORE_SWAP))
    x_rows = [h[:, :part] for h in halves]
    g_rows = [h[:, part + 128 :] for h in halves]
    tables = [h[:, part : part + 128] for h in halves]
    half = own.shape[0]
    blocks = half // toks
    w_gu = jnp.concatenate([a[: 2 * hid] for a in w], axis=0)
    w_d = jnp.concatenate([a[2 * hid :] for a in w], axis=0)

    pick = jnp.arange(128, dtype=jnp.int32)[:, None]
    owner = (jnp.arange(NX, dtype=jnp.int32)[None, :] * (experts - 2) + expert) % experts
    pick_own = ((pick % experts == expert) & (pick < 3 * experts)).astype(BF)
    unit = NX * toks
    token = jnp.arange(half, dtype=jnp.int32)[:, None]
    block = jnp.arange(blocks, dtype=jnp.int32)[None, :]
    y, z = lax.axis_index("dp") // NZ, lax.axis_index("dp") % NZ
    t_y, t_z = token // (NZ * unit), token // unit % NZ
    from_here = ((t_z + NZ - z) % NZ) * NY + (t_y + NY - y) % NY
    at = token // toks == block
    at_in_order = from_here * NX + token % unit // toks == block
    place, place_in_order, weight = [], [], []
    for table in tables:
        slots = [mm(table, (pick == owner + (3 + slot) * experts).astype(BF)) for slot in range(cap)]
        place.append([placing(at, [c[:, s : s + 1] for c in slots]) for s in range(NX)])
        slots = [in_order(a.reshape(NZ, NY, unit, NX), z, y).reshape(half, NX) for a in slots]
        place_in_order.append([placing(at_in_order, [c[:, s : s + 1] for c in slots]) for s in range(NX)])
        weight.append(jnp.sum(mm(table, pick_own) * place[-1][0].astype(F32), axis=0)[None])
    weight = jnp.concatenate(weight, axis=1)

    pre_gu = [nt(w_gu, h).astype(BF) for h in x_rows]
    pre_d = [nt(w_d, h).astype(BF) for h in g_rows]
    pre = []
    for s in range(NX):
        packed = [
            jnp.concatenate(
                [
                    mm(pre_gu[i][s * 2 * hid : (s + 1) * 2 * hid], place[i][s]),
                    mm(pre_d[i][s * hid : (s + 1) * hid], place[i][s]),
                ],
                axis=0,
            )
            for i in range(2)
        ]
        pre.append(shift_x(jnp.concatenate(packed, axis=1).astype(BF), -s))
    pre = sum(a.astype(F32) for a in pre)

    gate_pre, up_pre = pre[:hid], pre[hid : 2 * hid]
    delta_hidden = jnp.where(weight > 0.0, pre[2 * hid :] * weight, 0.0)
    sig_gate = jax.nn.sigmoid(gate_pre)
    silu_gate = gate_pre * sig_gate
    hidden = jnp.where(weight > 0.0, silu_gate * up_pre * weight, 0.0)
    delta_up = delta_hidden * silu_gate
    delta_gate = delta_hidden * up_pre * sig_gate * (1.0 + gate_pre * (1.0 - sig_gate))
    delta = jnp.concatenate([delta_gate, delta_up, hidden], axis=0).astype(BF)
    delta = [shift_x(delta, s) for s in range(NX)]
    d_gu, d_h, d_in_order = [], [], []
    for i in range(2):
        packed = [d[:, i * cap * blocks : (i + 1) * cap * blocks] for d in delta]
        d_in_order.append(
            jnp.concatenate([nt(d[: 2 * hid], place_in_order[i][s]) for s, d in enumerate(packed)], axis=0).astype(BF)
        )
        tokens_d = [nt(d, place[i][s]).astype(BF) for s, d in enumerate(packed)]
        d_gu.append(jnp.concatenate([d[: 2 * hid] for d in tokens_d], axis=0))
        d_h.append(jnp.concatenate([d[2 * hid :] for d in tokens_d], axis=0))

    theirs = lax.ppermute(tn(d_in_order[1], w_gu).astype(BF), "expert", CORE_SWAP)
    grad_x = (tn(d_in_order[0], w_gu) + theirs.astype(F32)).astype(BF)
    grad_x = lax.all_to_all(grad_x.reshape(NY * NZ, unit, part), "dp", 0, 0, tiled=True)
    grad_tokens = from_slices(across_x(total(grad_x).reshape(NX, toks, part)))

    g_gu = sum(mm(d_gu[i], h) for i, h in enumerate(x_rows)).astype(BF)
    g_d = sum(mm(d_h[i], h) for i, h in enumerate(g_rows)).astype(BF)
    g_all = [
        shift_x(
            jnp.concatenate(
                [g_gu[s * 2 * hid : (s + 1) * 2 * hid], g_d[s * hid : (s + 1) * hid]], axis=0
            ),
            -s,
        )
        for s in range(NX)
    ]
    grads = local_call(
        finish_kernel,
        NX + 1,
        [jax.ShapeDtypeStruct((1, hid, width), F32)] * 3,
        (3 * 3 * hid * width, 8 * 3 * hid * width),
    )(x_index, *g_all, keep)
    return (grad_tokens, *grads)


def solution(mesh):
    rows = P(("dp", "expert"), None)
    weights = P("expert", "dp", None)
    return jax.shard_map(
        per_device,
        mesh=mesh,
        in_specs=(rows,) * 4 + (weights,) * 6,
        out_specs=(rows,) + (weights,) * 3,
        check_vma=False,
    )
```

```python
import functools

import jax
import jax.numpy as jnp
from jax import lax
from jax.experimental import pallas as pl
from jax.experimental.pallas import tpu as pltpu
from jax.sharding import PartitionSpec as P

NX, NY, NZ = 4, 4, 8
GROUP = 32
X_GROUPS = [[0, 2, 4, 6], [1, 3, 5, 7]]
Z_GROUPS = [[y * NZ + z for z in range(NZ)] for y in range(NY)]
Z_ORDER = ((0, 1, 7, 2), (6, 3, 5, 4))
CORE_SWAP = [(i, i ^ 1) for i in range(8)]
BF = jnp.bfloat16
F32 = jnp.float32
VMEM_LIMIT = 60 * 1024 * 1024
KERNEL_VMEM = 24 * 1024 * 1024


def shift_x(a, by):
    if by % NX == 0:
        return a
    return lax.ppermute(a, "expert", [(i, ((i // 2 + by) % NX) * 2 + i % 2) for i in range(2 * NX)])


def shift_y(a, by):
    if by == 0:
        return a
    return lax.ppermute(a, "dp", [(i, ((i // NZ + by) % NY) * NZ + i % NZ) for i in range(NY * NZ)])


def shift_z(a, by):
    if by == 0:
        return a
    return lax.ppermute(a, "dp", [(i, (i // NZ) * NZ + (i % NZ + by) % NZ) for i in range(NY * NZ)])


def gather_y(a):
    return jnp.concatenate([a] + [shift_y(a, -k) for k in range(1, NY)], axis=0)


def gather_z(a, early, late, work):
    after, before = [a], [a]
    for step in range(NZ // 2 - 1):
        if step == 2:
            (after[-1], before[-1]), early = lax.optimization_barrier(((after[-1], before[-1]), early))
        after.append(shift_z(after[-1], -1))
        before.append(shift_z(before[-1], 1))
    last, late = lax.optimization_barrier(((after[-1], before[-1]), late))
    cut = a.shape[0] // 2
    far = (shift_z(last[0][:cut], -1), shift_z(last[1][cut:], 1))
    first = after[:3] + before[1:2]
    first = jnp.concatenate([first[0], first[1], first[3], first[2]], axis=0)
    first = (first, lax.ppermute(first, "expert", CORE_SWAP))
    partial, ws = work(first, early, late)
    far, mine = lax.optimization_barrier((far, partial[0]))
    done = ([mine, partial[1]], ws)
    second = jnp.concatenate([before[2], last[0], last[1], *far], axis=0)
    return first, done, (second, lax.ppermute(second, "expert", CORE_SWAP))


def by_y_and_z(a, z):
    flat = Z_ORDER[0] + Z_ORDER[1]
    a = a.reshape(NZ, NY, -1, a.shape[-1])
    a = jnp.concatenate([a[flat.index(k)][None] for k in range(NZ)] * 2, axis=0)
    a = lax.dynamic_slice_in_dim(a, NZ - z, NZ, 0)
    return a.transpose(1, 0, 2, 3).reshape(-1, a.shape[-1])


def total(terms):
    return sum(a.astype(F32) for a in terms).astype(BF)


def exchange(a, groups):
    return lax.all_to_all(a, "dp", 0, 0, axis_index_groups=groups, tiled=True)


def across_x(a):
    return lax.all_to_all(a, "expert", 0, 0, axis_index_groups=X_GROUPS, tiled=True)


def to_slices(a):
    return a.reshape(a.shape[0], NX, -1).transpose(1, 0, 2)


def from_slices(a):
    return a.transpose(1, 0, 2).reshape(a.shape[1], -1)


def nt(a, b):
    return lax.dot_general(a, b, (((1,), (1,)), ((), ())), preferred_element_type=F32)


def tn(a, b):
    return lax.dot_general(a, b, (((0,), (0,)), ((), ())), preferred_element_type=F32)


def mm(a, b):
    return jnp.dot(a, b, preferred_element_type=F32)


def three_terms(a):
    hi = a.astype(BF)
    rest = a - hi.astype(F32)
    mid = rest.astype(BF)
    return hi, mid, (rest - mid.astype(F32)).astype(BF)


def dequantize_kernel(x_ref, gm, um, dm, gs, us, ds, w0, w1, w2, w3, keep):
    step = pl.program_id(0)
    hid, groups = gs.shape[1:]
    part = w0.shape[1]
    scales = three_terms(jnp.concatenate([gs[0], us[0], ds[0]], axis=0))
    group = lax.broadcasted_iota(jnp.int32, (groups, part), 0)
    lane_group = lax.broadcasted_iota(jnp.int32, (groups, part), 1) // GROUP
    first = lax.rem(x_ref[0] + step, NX) * (part // GROUP)
    spread = jnp.where(group == lane_group + first, 1.0, 0.0).astype(BF)
    scale = mm(scales[0], spread) + mm(scales[1], spread) + mm(scales[2], spread)
    for p, master in enumerate((gm, um, dm)):
        rows = slice(p * hid, (p + 1) * hid)
        unit = scale[rows]
        ratio = master[0] / unit
        levels = jnp.clip(jnp.floor(ratio + 0.5), -8.0, 7.0)
        weight = (levels * unit).astype(BF)
        for s, w in enumerate((w0, w1, w2, w3)):

            @pl.when(step == s)
            def _(w=w, weight=weight, rows=rows):
                w[rows] = weight

        keep[0, rows] = jnp.where((ratio > -8.5) & (ratio < 7.5), 1.0, 0.0).astype(BF)


def dequantize(x_index, masters, scales):
    _, hid, width = masters[0].shape
    part = width // NX
    grid = pltpu.PrefetchScalarGridSpec(
        num_scalar_prefetch=1,
        grid=(NX,),
        in_specs=[pl.BlockSpec((1, hid, part), lambda i, x: (0, 0, lax.rem(x[0] + i, NX)))] * 3
        + [pl.BlockSpec(scales[0].shape, lambda i, x: (0, 0, 0))] * 3,
        out_specs=[pl.BlockSpec((3 * hid, part), lambda i, x: (0, 0))] * NX
        + [pl.BlockSpec((1, 3 * hid, part), lambda i, x: (i, 0, 0))],
    )
    return pl.pallas_call(
        dequantize_kernel,
        grid_spec=grid,
        out_shape=[jax.ShapeDtypeStruct((3 * hid, part), BF)] * NX
        + [jax.ShapeDtypeStruct((NX, 3 * hid, part), BF)],
        compiler_params=pltpu.CompilerParams(vmem_limit_bytes=VMEM_LIMIT),
        cost_estimate=pl.CostEstimate(
            flops=30 * 3 * hid * width, bytes_accessed=8 * 3 * hid * width, transcendentals=0
        ),
    )(x_index, *masters, *scales)


def finish_kernel(x_ref, r0, r1, r2, r3, keep, og, ou, od):
    hid = og.shape[1]
    part = r0.shape[1]
    for s, r in enumerate((r0, r1, r2, r3)):
        col = pl.multiple_of(lax.rem(x_ref[0] + s, NX) * part, 128)
        for p, out in enumerate((og, ou, od)):
            rows = slice(p * hid, (p + 1) * hid)
            out[0, :, pl.ds(col, part)] = jnp.where(
                keep[s, rows].astype(F32) > 0.0, r[rows].astype(F32), 0.0
            )


def slot_of(found, blocks, toks, s):
    block = lax.broadcasted_iota(jnp.int32, (found.shape[0], 1), 0) // toks
    second = jnp.where(found[:, 2 * s + 1 : 2 * s + 2] > 0.5, block + blocks, -1)
    return jnp.where(found[:, 2 * s : 2 * s + 1] > 0.5, block, second)


def places(slot, slots):
    column = lax.broadcasted_iota(jnp.int32, (slot.shape[0], slots), 1)
    return jnp.where(column == slot, 1.0, 0.0)


def forward_kernel(toks, rows, pick, w0, w1, w2, w3, p0, p1, p2, p3, weight, slot):
    ws, outs = (w0, w1, w2, w3), (p0, p1, p2, p3)
    part, n, slots = w0.shape[1], rows.shape[0], weight.shape[1]
    gu = 2 * w0.shape[0] // 3
    found = mm(rows[:, 2 * part :], pick[...])
    x, g = rows[:, :part], rows[:, part : 2 * part]
    pre_gu = nt(jnp.concatenate([w[:gu] for w in ws], axis=0), x).astype(BF)
    pre_d = nt(jnp.concatenate([w[gu:] for w in ws], axis=0), g).astype(BF)
    slot[...] = jnp.full(slot.shape, -1, jnp.int32)
    for s, out in enumerate(outs):
        where = slot_of(found, n // toks, toks, s)
        slot[:, s : s + 1] = where
        place = places(where, slots)
        if s == 0:
            weight[...] = jnp.sum(place * found[:, 8:9], axis=0, keepdims=True)
        place = place.astype(BF)
        out[:gu] = mm(pre_gu[s * gu : (s + 1) * gu], place).astype(BF)
        out[gu:] = mm(pre_d[s * gu // 2 : (s + 1) * gu // 2], place).astype(BF)


def weight_grad_kernel(
    s0, s1, s2, s3, x0, x1, x2, x3, g0, g1, g2, g3, d0, d1, d2, d3, o0, o1, o2, o3, d_gu, d_h
):
    ds, outs = (d0, d1, d2, d3), (o0, o1, o2, o3)
    gu = 2 * o0.shape[0] // 3
    slots = d0.shape[1] // 4

    @pl.when(pl.program_id(0) == 0)
    def _():
        for i, slot in enumerate((s0, s1, s2, s3)):
            for s, d in enumerate(ds):
                spread = nt(
                    d[:, i * slots : (i + 1) * slots], places(slot[:, s : s + 1], slots).astype(BF)
                ).astype(BF)
                at = slice(i * spread.shape[1], (i + 1) * spread.shape[1])
                d_gu[s * gu : (s + 1) * gu, at] = spread[:gu]
                d_h[s * gu // 2 : (s + 1) * gu // 2, at] = spread[gu:]

    x = jnp.concatenate([x0[...], x1[...], x2[...], x3[...]], axis=0)
    g = jnp.concatenate([g0[...], g1[...], g2[...], g3[...]], axis=0)
    g_gu = mm(d_gu[...], x).astype(BF)
    g_h = mm(d_h[...], g).astype(BF)
    for s, out in enumerate(outs):
        out[:gu] = g_gu[s * gu : (s + 1) * gu]
        out[gu:] = g_h[s * gu // 2 : (s + 1) * gu // 2]


def weight_grads(slots, groups, delta, part):
    n, rows = groups[0].shape[0], delta[0].shape[0]
    wide = 256 if part % 256 == 0 else part
    first, second = part // wide, 2 * rows // 3
    whole = lambda a: pl.BlockSpec(a.shape, lambda i: (0, 0))
    return pl.pallas_call(
        weight_grad_kernel,
        grid=(first,),
        out_shape=[jax.ShapeDtypeStruct((rows, part), BF)] * NX,
        in_specs=[whole(a) for a in slots]
        + [pl.BlockSpec((n, wide), lambda i: (0, i))] * 4
        + [pl.BlockSpec((n, wide), lambda i: (0, first + i))] * 4
        + [whole(a) for a in delta],
        out_specs=[pl.BlockSpec((rows, wide), lambda i: (0, i))] * NX,
        scratch_shapes=[pltpu.VMEM((NX * second, 4 * n), BF), pltpu.VMEM((NX * second // 2, 4 * n), BF)],
        compiler_params=pltpu.CompilerParams(vmem_limit_bytes=VMEM_LIMIT),
        cost_estimate=pl.CostEstimate(
            flops=2 * rows * NX * part * 4 * n,
            bytes_accessed=2 * (8 * n * part + 2 * NX * rows * part),
            transcendentals=0,
        ),
    )(*slots, *groups, *groups, *delta)


def input_grad(half, slot, ds, ws):
    gu = 2 * ws[0].shape[0] // 3
    slots = ds[0].shape[1] // 2
    spread = jnp.concatenate(
        [
            nt(places(slot[:, s : s + 1], slots).astype(BF), d[:gu, half * slots : (half + 1) * slots])
            for s, d in enumerate(ds)
        ],
        axis=1,
    ).astype(BF)
    return mm(spread, jnp.concatenate([w[:gu] for w in ws], axis=0))


def theirs_kernel(slot, d0, d1, d2, d3, w0, w1, w2, w3, out):
    out[...] = input_grad(1, slot, (d0, d1, d2, d3), (w0, w1, w2, w3)).astype(BF)


def ours_kernel(slot, d0, d1, d2, d3, w0, w1, w2, w3, theirs, l0, l1, l2, l3, right):
    grad = input_grad(0, slot, (d0, d1, d2, d3), (w0, w1, w2, w3))
    grad = (grad + theirs[...].astype(F32)).astype(BF)
    cut = l0.shape[1]
    unit = grad.shape[0] // (NY * NZ)
    for y, left in enumerate((l0, l1, l2, l3)):
        left[...] = grad[y * NZ * unit : (y + 1) * NZ * unit, :cut]
        for z in range(NZ):
            row = (y * NZ + z) * unit
            right[z, y * unit : (y + 1) * unit] = grad[row : row + unit, cut:]


def local_call(kernel, out_shape, cost, scalars=0, limit=KERNEL_VMEM):
    vmem = pl.BlockSpec(memory_space=pltpu.VMEM)
    smem = pl.BlockSpec(memory_space=pltpu.SMEM)

    def call(*args):
        return pl.pallas_call(
            kernel,
            out_shape=out_shape,
            in_specs=[smem] * scalars + [vmem] * (len(args) - scalars),
            out_specs=[vmem] * len(out_shape),
            compiler_params=pltpu.CompilerParams(vmem_limit_bytes=limit),
            cost_estimate=pl.CostEstimate(flops=cost[0], bytes_accessed=cost[1], transcendentals=0),
        )(*args)

    return call


def per_device(
    tokens,
    grad_out,
    expert_ids,
    gate_values,
    gate_master,
    gate_scale,
    up_master,
    up_scale,
    down_master,
    down_scale,
):
    experts = lax.axis_size("expert")
    expert = lax.axis_index("expert")
    toks, width = tokens.shape
    hid = gate_master.shape[1]
    part = width // NX
    cap = toks // 2
    x_index = (expert // 2).reshape(1)

    named = expert_ids[:, :, None] == jnp.arange(experts, dtype=jnp.int32)
    factor = jnp.sum(jnp.where(named, gate_values[:, :, None], 0.0), axis=1)
    member = jnp.any(named, axis=1)
    rank = jnp.cumsum(member.astype(jnp.int32), axis=0) - 1
    f_hi = lax.reduce_precision(factor, 8, 7)
    f_mid = lax.reduce_precision(factor - f_hi, 8, 7)
    cols = [f_hi, f_mid, factor - f_hi - f_mid]
    cols += [jnp.where(member & (rank == slot), 1.0, 0.0) for slot in range(cap)]
    cols = jnp.concatenate(cols, axis=1).astype(BF)
    cols = jnp.pad(cols, ((0, 0), (0, 128 - cols.shape[1])))
    payload = jnp.concatenate(
        [to_slices(tokens), to_slices(grad_out), jnp.broadcast_to(cols, (NX,) + cols.shape)], axis=2
    )
    mine = across_x(payload).reshape(NX * toks, -1)
    *w_mine, keep = dequantize(
        x_index, (gate_master, up_master, down_master), (gate_scale, up_scale, down_scale)
    )
    own, w_mine = lax.optimization_barrier((gather_y(mine), w_mine))
    w = [shift_x(a, s) if s != 2 else a for s, a in enumerate(w_mine)]
    w = lax.optimization_barrier(w)
    n = NY * NZ * NX * toks // 2
    slots = n // toks * cap

    row = jnp.arange(128, dtype=jnp.int32)[:, None]
    col = jnp.arange(128, dtype=jnp.int32)[None, :]
    owner = (col // cap * (experts - 2) + expert) % experts
    pick = (col < cap * NX) & (row == owner + (3 + col % cap) * experts)
    pick |= (col == cap * NX) & (row % experts == expert) & (row < 3 * experts)
    pick = pick.astype(BF)
    row_bytes = 2 * n * mine.shape[1]
    w_bytes = 2 * 3 * hid * width
    forward = local_call(
        functools.partial(forward_kernel, toks),
        [jax.ShapeDtypeStruct((3 * hid, slots), BF)] * NX
        + [jax.ShapeDtypeStruct((1, slots), F32), jax.ShapeDtypeStruct((n, 128), jnp.int32)],
        (2 * 3 * hid * width * n, row_bytes + w_bytes),
    )

    def work(rows, early, late):
        ws = (w[0], early[0], late, early[1])
        return [forward(a, pick, *ws) for a in rows], ws

    first, (partial, w), second = gather_z(own, (w[1], w[3]), shift_x(w[2], 2), work)
    partial = partial + [forward(a, pick, *w) for a in second]
    groups = [first[0], second[0], first[1], second[1]]
    partial = [partial[i] for i in (0, 2, 1, 3)]
    weight = jnp.concatenate([p[NX] for p in partial], axis=1)
    pre = [shift_x(jnp.concatenate([p[s] for p in partial], axis=1), -s) for s in range(NX)]
    slot = [p[NX + 1] for p in partial]
    by_half = [jnp.where(a >= 0, a + i % 2 * slots, -1) for i, a in enumerate(slot)]
    z = lax.axis_index("dp") % NZ
    by_half = [by_y_and_z(jnp.concatenate(by_half[i : i + 2], axis=0), z) for i in (0, 2)]

    pre = sum(a.astype(F32) for a in pre)

    gate_pre, up_pre = pre[:hid], pre[hid : 2 * hid]
    delta_hidden = jnp.where(weight > 0.0, pre[2 * hid :] * weight, 0.0)
    sig_gate = jax.nn.sigmoid(gate_pre)
    silu_gate = gate_pre * sig_gate
    hidden = jnp.where(weight > 0.0, silu_gate * up_pre * weight, 0.0)
    delta_up = delta_hidden * silu_gate
    delta_gate = delta_hidden * up_pre * sig_gate * (1.0 + gate_pre * (1.0 - sig_gate))
    delta = jnp.concatenate([delta_gate, delta_up, hidden], axis=0).astype(BF)
    delta = [shift_x(delta, s) for s in range(NX)]
    half = 2 * n
    theirs = local_call(
        theirs_kernel,
        [jax.ShapeDtypeStruct((half, part), BF)],
        (4 * hid * width * half, row_bytes + w_bytes),
    )(by_half[1], *delta, *w)[0]
    theirs = lax.ppermute(theirs, "expert", CORE_SWAP)
    g_all = weight_grads(slot, groups, delta, part)
    cut = part * 5 // 7
    unit = NX * toks
    *left, right = local_call(
        ours_kernel,
        [
            *[jax.ShapeDtypeStruct((NZ * unit, cut), BF)] * NY,
            jax.ShapeDtypeStruct((NZ, NY * unit, part - cut), BF),
        ],
        (4 * hid * width * half, 2 * row_bytes + w_bytes),
    )(by_half[0], *delta, *w, theirs)
    right = exchange(right, Z_GROUPS)
    left, _ = lax.optimization_barrier(([shift_y(left[k], k) for k in range(NY)], g_all))
    near, third = lax.optimization_barrier(((shift_x(g_all[1], -1), shift_x(g_all[3], -3)), g_all[2]))
    left = total(left).reshape(NZ, unit, cut)
    right = total(list(right)).reshape(NY, unit, part - cut)
    left = total(list(exchange(left, Z_GROUPS)))
    right = total([shift_y(right[k], k) for k in range(NY)])
    grad_x = jnp.concatenate([left, right], axis=1)
    third = shift_x(third, -2)
    grad_tokens = from_slices(across_x(grad_x.reshape(NX, toks, part)))

    g_all = (g_all[0], near[0], third, near[1])
    grads = local_call(
        finish_kernel,
        [jax.ShapeDtypeStruct((1, hid, width), F32)] * 3,
        (3 * 3 * hid * width, 8 * 3 * hid * width),
        scalars=1,
    )(x_index, *g_all, keep)
    return (grad_tokens, *grads)


def solution(mesh):
    rows = P(("dp", "expert"), None)
    weights = P("expert", "dp", None)
    return jax.shard_map(
        per_device,
        mesh=mesh,
        in_specs=(rows,) * 4 + (weights,) * 6,
        out_specs=(rows,) + (weights,) * 3,
        check_vma=False,
    )
```

```python
import functools

import jax
import jax.numpy as jnp
from jax import lax
from jax.experimental import pallas as pl
from jax.experimental.pallas import tpu as pltpu
from jax.sharding import PartitionSpec as P

NX, NY, NZ = 4, 4, 8
GROUP = 32
Z_ORDER = ((0, 1, 7, 2), (6, 3, 5, 4))
AXES = ("y", "z", "x", "core")
BF = jnp.bfloat16
F32 = jnp.float32
VMEM_LIMIT = 60 * 1024 * 1024
KERNEL_VMEM = 24 * 1024 * 1024


def shift(a, axis, by):
    size = lax.axis_size(axis)
    if by % size == 0:
        return a
    return lax.ppermute(a, axis, [(i, (i + by) % size) for i in range(size)])


def gather_z(a, early, late, work):
    after, before = [a], [a]
    for step in range(NZ // 2 - 1):
        if step == 2:
            (after[-1], before[-1]), early = lax.optimization_barrier(((after[-1], before[-1]), early))
        after.append(shift(after[-1], "z", -1))
        before.append(shift(before[-1], "z", 1))
    last, late = lax.optimization_barrier(((after[-1], before[-1]), late))
    cut = a.shape[0] // 2
    far = (shift(last[0][:cut], "z", -1), shift(last[1][cut:], "z", 1))
    first = after[:3] + before[1:2]
    first = jnp.concatenate([first[0], first[1], first[3], first[2]], axis=0)
    first = (first, shift(first, "core", 1))
    partial, ws = work(first, early, late)
    far, mine = lax.optimization_barrier((far, partial[0]))
    done = ([mine, partial[1]], ws)
    second = jnp.concatenate([before[2], last[0], last[1], *far], axis=0)
    return first, done, (second, shift(second, "core", 1))


def by_y_and_z(a, z):
    flat = Z_ORDER[0] + Z_ORDER[1]
    a = a.reshape(NZ, NY, -1, a.shape[-1])
    a = jnp.concatenate([a[flat.index(k)][None] for k in range(NZ)] * 2, axis=0)
    a = lax.dynamic_slice_in_dim(a, NZ - z, NZ, 0)
    return a.transpose(1, 0, 2, 3).reshape(-1, a.shape[-1])


def total(terms):
    return sum(a.astype(F32) for a in terms).astype(BF)


def exchange(a, axes):
    return lax.all_to_all(a, axes, 0, 0, tiled=True)


def to_slices(a):
    return a.reshape(a.shape[0], NX, -1).transpose(1, 0, 2)


def from_slices(a):
    return a.transpose(1, 0, 2).reshape(a.shape[1], -1)


def nt(a, b):
    return lax.dot_general(a, b, (((1,), (1,)), ((), ())), preferred_element_type=F32)


def tn(a, b):
    return lax.dot_general(a, b, (((0,), (0,)), ((), ())), preferred_element_type=F32)


def mm(a, b):
    return jnp.dot(a, b, preferred_element_type=F32)


def three_terms(a):
    hi = a.astype(BF)
    rest = a - hi.astype(F32)
    mid = rest.astype(BF)
    return hi, mid, (rest - mid.astype(F32)).astype(BF)


def dequantize_kernel(x_ref, gm, um, dm, gs, us, ds, w0, w1, w2, w3, keep):
    step = pl.program_id(0)
    hid, groups = gs.shape[1:]
    part = w0.shape[1]
    scales = three_terms(jnp.concatenate([gs[0], us[0], ds[0]], axis=0))
    group = lax.broadcasted_iota(jnp.int32, (groups, part), 0)
    lane_group = lax.broadcasted_iota(jnp.int32, (groups, part), 1) // GROUP
    first = lax.rem(x_ref[0] + step, NX) * (part // GROUP)
    spread = jnp.where(group == lane_group + first, 1.0, 0.0).astype(BF)
    scale = mm(scales[0], spread) + mm(scales[1], spread) + mm(scales[2], spread)
    for p, master in enumerate((gm, um, dm)):
        rows = slice(p * hid, (p + 1) * hid)
        unit = scale[rows]
        ratio = master[0] / unit
        levels = jnp.clip(jnp.floor(ratio + 0.5), -8.0, 7.0)
        weight = (levels * unit).astype(BF)
        for s, w in enumerate((w0, w1, w2, w3)):

            @pl.when(step == s)
            def _(w=w, weight=weight, rows=rows):
                w[rows] = weight

        keep[0, rows] = jnp.where((ratio > -8.5) & (ratio < 7.5), 1.0, 0.0).astype(BF)


def dequantize(x_index, masters, scales):
    _, hid, width = masters[0].shape
    part = width // NX
    grid = pltpu.PrefetchScalarGridSpec(
        num_scalar_prefetch=1,
        grid=(NX,),
        in_specs=[pl.BlockSpec((1, hid, part), lambda i, x: (0, 0, lax.rem(x[0] + i, NX)))] * 3
        + [pl.BlockSpec(scales[0].shape, lambda i, x: (0, 0, 0))] * 3,
        out_specs=[pl.BlockSpec((3 * hid, part), lambda i, x: (0, 0))] * NX
        + [pl.BlockSpec((1, 3 * hid, part), lambda i, x: (i, 0, 0))],
    )
    return pl.pallas_call(
        dequantize_kernel,
        grid_spec=grid,
        out_shape=[jax.ShapeDtypeStruct((3 * hid, part), BF)] * NX
        + [jax.ShapeDtypeStruct((NX, 3 * hid, part), BF)],
        compiler_params=pltpu.CompilerParams(vmem_limit_bytes=VMEM_LIMIT),
        cost_estimate=pl.CostEstimate(
            flops=30 * 3 * hid * width, bytes_accessed=8 * 3 * hid * width, transcendentals=0
        ),
    )(x_index, *masters, *scales)


def finish_kernel(x_ref, r0, r1, r2, r3, keep, og, ou, od):
    hid = og.shape[1]
    part = r0.shape[1]
    for s, r in enumerate((r0, r1, r2, r3)):
        col = pl.multiple_of(lax.rem(x_ref[0] + s, NX) * part, 128)
        for p, out in enumerate((og, ou, od)):
            rows = slice(p * hid, (p + 1) * hid)
            out[0, :, pl.ds(col, part)] = jnp.where(
                keep[s, rows].astype(F32) > 0.0, r[rows].astype(F32), 0.0
            )


def slot_of(found, blocks, toks, s):
    block = lax.broadcasted_iota(jnp.int32, (found.shape[0], 1), 0) // toks
    second = jnp.where(found[:, 2 * s + 1 : 2 * s + 2] > 0.5, block + blocks, -1)
    return jnp.where(found[:, 2 * s : 2 * s + 1] > 0.5, block, second)


def places(slot, slots):
    column = lax.broadcasted_iota(jnp.int32, (slot.shape[0], slots), 1)
    return jnp.where(column == slot, 1.0, 0.0)


def forward_kernel(toks, rows, pick, w0, w1, w2, w3, p0, p1, p2, p3, weight, slot):
    ws, outs = (w0, w1, w2, w3), (p0, p1, p2, p3)
    part, n, slots = w0.shape[1], rows.shape[0], weight.shape[1]
    gu = 2 * w0.shape[0] // 3
    found = mm(rows[:, 2 * part :], pick[...])
    x, g = rows[:, :part], rows[:, part : 2 * part]
    pre_gu = nt(jnp.concatenate([w[:gu] for w in ws], axis=0), x).astype(BF)
    pre_d = nt(jnp.concatenate([w[gu:] for w in ws], axis=0), g).astype(BF)
    slot[...] = jnp.full(slot.shape, -1, jnp.int32)
    for s, out in enumerate(outs):
        where = slot_of(found, n // toks, toks, s)
        slot[:, s : s + 1] = where
        place = places(where, slots)
        if s == 0:
            weight[...] = jnp.sum(place * found[:, 8:9], axis=0, keepdims=True)
        place = place.astype(BF)
        out[:gu] = mm(pre_gu[s * gu : (s + 1) * gu], place).astype(BF)
        out[gu:] = mm(pre_d[s * gu // 2 : (s + 1) * gu // 2], place).astype(BF)


def weight_grad_kernel(
    experts, s0, s1, s2, s3, da, db, r0, r1, r2, r3, oa, ob, x, g, d_gu, d_h, sems
):
    gu = 2 * oa.shape[0] // 3
    slots = da.shape[1] // 4
    n, part = r0.shape[0], oa.shape[1]
    copies = [
        pltpu.make_async_copy(
            r.at[:, pl.ds(k * part, part)], dst.at[pl.ds(i * n, n)], sems.at[4 * k + i]
        )
        for k, dst in enumerate((x, g))
        for i, r in enumerate((r0, r1, r2, r3))
    ]
    for copy in copies:
        copy.start()
    for i, slot in enumerate((s0, s1, s2, s3)):
        for j, (s, d) in enumerate(zip(experts, (da, db))):
            spread = nt(
                d[:, i * slots : (i + 1) * slots], places(slot[:, s : s + 1], slots).astype(BF)
            ).astype(BF)
            at = slice(i * n, (i + 1) * n)
            d_gu[j * gu : (j + 1) * gu, at] = spread[:gu]
            d_h[j * gu // 2 : (j + 1) * gu // 2, at] = spread[gu:]
    for copy in copies[:4]:
        copy.wait()
    grad = mm(d_gu[...], x[...]).astype(BF)
    oa[:gu] = grad[:gu]
    ob[:gu] = grad[gu:]
    for copy in copies[4:]:
        copy.wait()
    grad = mm(d_h[...], g[...]).astype(BF)
    oa[gu:] = grad[: gu // 2]
    ob[gu:] = grad[gu // 2 :]


def weight_grads(experts, slots, groups, delta, part):
    n, rows = groups[0].shape[0], delta[0].shape[0]
    gu = 2 * rows // 3
    vmem = pl.BlockSpec(memory_space=pltpu.VMEM)
    return pl.pallas_call(
        functools.partial(weight_grad_kernel, experts),
        out_shape=[jax.ShapeDtypeStruct((rows, part), BF)] * 2,
        in_specs=[vmem] * 6 + [pl.BlockSpec(memory_space=pl.ANY)] * 4,
        out_specs=[vmem] * 2,
        scratch_shapes=[
            pltpu.VMEM((4 * n, part), BF),
            pltpu.VMEM((4 * n, part), BF),
            pltpu.VMEM((2 * gu, 4 * n), BF),
            pltpu.VMEM((gu, 4 * n), BF),
            pltpu.SemaphoreType.DMA((8,)),
        ],
        compiler_params=pltpu.CompilerParams(vmem_limit_bytes=KERNEL_VMEM),
        cost_estimate=pl.CostEstimate(
            flops=2 * rows * 2 * part * 4 * n,
            bytes_accessed=2 * (8 * n * part + 2 * 2 * rows * part),
            transcendentals=0,
        ),
    )(*slots, *[delta[s] for s in experts], *groups)


def input_grad(half, slot, ds, ws):
    gu = 2 * ws[0].shape[0] // 3
    slots = ds[0].shape[1] // 2
    spread = jnp.concatenate(
        [
            nt(places(slot[:, s : s + 1], slots).astype(BF), d[:gu, half * slots : (half + 1) * slots])
            for s, d in enumerate(ds)
        ],
        axis=1,
    ).astype(BF)
    return mm(spread, jnp.concatenate([w[:gu] for w in ws], axis=0))


def theirs_kernel(slot, d0, d1, d2, d3, w0, w1, w2, w3, out):
    out[...] = input_grad(1, slot, (d0, d1, d2, d3), (w0, w1, w2, w3)).astype(BF)


def ours_kernel(y_ref, slot, d0, d1, d2, d3, w0, w1, w2, w3, theirs, o0, o1, o2, o3, grad):
    total_grad = input_grad(0, slot, (d0, d1, d2, d3), (w0, w1, w2, w3)) + theirs[...].astype(F32)
    grad[...] = total_grad.astype(BF)
    rows = o0.shape[0]
    for k, out in enumerate((o0, o1, o2, o3)):
        start = pl.multiple_of(lax.rem(y_ref[0] + k, NY) * rows, rows)
        out[...] = grad[pl.ds(start, rows), :]


def local_call(kernel, out_shape, cost, scalars=0, scratch=()):
    vmem = pl.BlockSpec(memory_space=pltpu.VMEM)
    smem = pl.BlockSpec(memory_space=pltpu.SMEM)

    def call(*args):
        return pl.pallas_call(
            kernel,
            out_shape=out_shape,
            in_specs=[smem] * scalars + [vmem] * (len(args) - scalars),
            out_specs=[vmem] * len(out_shape),
            scratch_shapes=list(scratch),
            compiler_params=pltpu.CompilerParams(vmem_limit_bytes=KERNEL_VMEM),
            cost_estimate=pl.CostEstimate(flops=cost[0], bytes_accessed=cost[1], transcendentals=0),
        )(*args)

    return call


def per_device(
    tokens,
    grad_out,
    expert_ids,
    gate_values,
    gate_master,
    gate_scale,
    up_master,
    up_scale,
    down_master,
    down_scale,
):
    x, y, z = (lax.axis_index(name) for name in ("x", "y", "z"))
    experts = NX * lax.axis_size("core")
    expert = x * lax.axis_size("core") + lax.axis_index("core")
    toks, width = tokens.shape
    hid = gate_master.shape[1]
    part = width // NX
    cap = toks // 2
    x_index = x.reshape(1)

    named = expert_ids[:, :, None] == jnp.arange(experts, dtype=jnp.int32)
    factor = jnp.sum(jnp.where(named, gate_values[:, :, None], 0.0), axis=1)
    member = jnp.any(named, axis=1)
    rank = jnp.cumsum(member.astype(jnp.int32), axis=0) - 1
    f_hi = lax.reduce_precision(factor, 8, 7)
    f_mid = lax.reduce_precision(factor - f_hi, 8, 7)
    cols = [f_hi, f_mid, factor - f_hi - f_mid]
    cols += [jnp.where(member & (rank == slot), 1.0, 0.0) for slot in range(cap)]
    cols = jnp.concatenate(cols, axis=1).astype(BF)
    cols = jnp.pad(cols, ((0, 0), (0, 128 - cols.shape[1])))
    payload = jnp.concatenate(
        [to_slices(tokens), to_slices(grad_out), jnp.broadcast_to(cols, (NX,) + cols.shape)], axis=2
    )
    payload = jnp.broadcast_to(payload, (NY,) + payload.shape).reshape(NY * NX, toks, -1)
    own = exchange(payload, ("y", "x")).reshape(NY * NX * toks, -1)
    *w_mine, keep = dequantize(
        x_index, (gate_master, up_master, down_master), (gate_scale, up_scale, down_scale)
    )
    own, w_mine = lax.optimization_barrier((own, w_mine))
    w = [shift(a, "x", s) if s != 2 else a for s, a in enumerate(w_mine)]
    w = lax.optimization_barrier(w)
    n = NY * NZ * NX * toks // 2
    slots = n // toks * cap

    row = jnp.arange(128, dtype=jnp.int32)[:, None]
    col = jnp.arange(128, dtype=jnp.int32)[None, :]
    owner = (col // cap * (experts - 2) + expert) % experts
    pick = (col < cap * NX) & (row == owner + (3 + col % cap) * experts)
    pick |= (col == cap * NX) & (row % experts == expert) & (row < 3 * experts)
    pick = pick.astype(BF)
    row_bytes = 2 * n * own.shape[1]
    w_bytes = 2 * 3 * hid * width
    forward = local_call(
        functools.partial(forward_kernel, toks),
        [jax.ShapeDtypeStruct((3 * hid, slots), BF)] * NX
        + [jax.ShapeDtypeStruct((1, slots), F32), jax.ShapeDtypeStruct((n, 128), jnp.int32)],
        (2 * 3 * hid * width * n, row_bytes + w_bytes),
    )

    def work(rows, early, late):
        ws = (w[0], early[0], late, early[1])
        return [forward(a, pick, *ws) for a in rows], ws

    first, (partial, w), second = gather_z(own, (w[1], w[3]), shift(w[2], "x", 2), work)
    partial = partial + [forward(a, pick, *w) for a in second]
    groups = [first[0], second[0], first[1], second[1]]
    partial = [partial[i] for i in (0, 2, 1, 3)]
    weight = jnp.concatenate([p[NX] for p in partial], axis=1)
    pre = [shift(jnp.concatenate([p[s] for p in partial], axis=1), "x", -s) for s in range(NX)]
    slot = [p[NX + 1] for p in partial]
    by_half = [jnp.where(a >= 0, a + i % 2 * slots, -1) for i, a in enumerate(slot)]
    by_half = [by_y_and_z(jnp.concatenate(by_half[i : i + 2], axis=0), z) for i in (0, 2)]

    pre = sum(a.astype(F32) for a in pre)

    gate_pre, up_pre = pre[:hid], pre[hid : 2 * hid]
    delta_hidden = jnp.where(weight > 0.0, pre[2 * hid :] * weight, 0.0)
    sig_gate = jax.nn.sigmoid(gate_pre)
    silu_gate = gate_pre * sig_gate
    hidden = jnp.where(weight > 0.0, silu_gate * up_pre * weight, 0.0)
    delta_up = delta_hidden * silu_gate
    delta_gate = delta_hidden * up_pre * sig_gate * (1.0 + gate_pre * (1.0 - sig_gate))
    delta = jnp.concatenate([delta_gate, delta_up, hidden], axis=0).astype(BF)
    delta = [shift(delta, "x", s) for s in range(NX)]
    half = 2 * n
    theirs = local_call(
        theirs_kernel,
        [jax.ShapeDtypeStruct((half, part), BF)],
        (4 * hid * width * half, row_bytes + w_bytes),
    )(by_half[1], *delta, *w)[0]
    theirs = shift(theirs, "core", 1)
    g_near = weight_grads((1, 3), slot, groups, delta, part)
    theirs, g_near = lax.optimization_barrier((theirs, g_near))
    near = (shift(g_near[0], "x", -1), shift(g_near[1], "x", -3))
    g_own, g_far = weight_grads((0, 2), slot, groups, delta, part)
    unit = NX * toks
    grad_x = local_call(
        ours_kernel,
        [jax.ShapeDtypeStruct((NZ * unit, part), BF)] * NY,
        (4 * hid * width * half, 2 * row_bytes + w_bytes),
        scalars=1,
        scratch=[pltpu.VMEM((half, part), BF)],
    )(y.reshape(1), by_half[0], *delta, *w, theirs)
    grad_x = [shift(g, "y", k) for k, g in enumerate(grad_x)]
    near, g_far = lax.optimization_barrier((near, g_far))
    far = shift(g_far, "x", -2)
    grad_x = total(grad_x).reshape(NZ * NX, toks, part)
    grad_x, far = lax.optimization_barrier((grad_x, far))
    grad_x = exchange(grad_x, ("z", "x"))
    grad_tokens = from_slices(total(list(grad_x.reshape(NZ, NX, toks, part))))

    g_all = (g_own, near[0], far, near[1])
    grads = local_call(
        finish_kernel,
        [jax.ShapeDtypeStruct((1, hid, width), F32)] * 3,
        (3 * 3 * hid * width, 8 * 3 * hid * width),
        scalars=1,
    )(x_index, *g_all, keep)
    return (grad_tokens, *grads)


def solution(mesh):
    mesh = jax.sharding.Mesh(mesh.devices.reshape(NY, NZ, NX, -1), AXES)
    rows = P(AXES, None)
    weights = P(("x", "core"), ("y", "z"), None)
    return jax.shard_map(
        per_device,
        mesh=mesh,
        in_specs=(rows,) * 4 + (weights,) * 6,
        out_specs=(rows,) + (weights,) * 3,
        check_vma=False,
    )
```

```python
import functools

import jax
import jax.numpy as jnp
from jax import lax
from jax.experimental import pallas as pl
from jax.experimental.pallas import tpu as pltpu
from jax.sharding import PartitionSpec as P

NX, NY, NZ = 4, 4, 8
GROUP = 32
Z_ORDER = ((0, 1, 7, 2), (6, 3, 5, 4))
AXES = ("y", "z", "x", "core")
BF = jnp.bfloat16
F32 = jnp.float32
VMEM_LIMIT = 60 * 1024 * 1024
KERNEL_VMEM = 24 * 1024 * 1024


def shift(a, axis, by):
    size = lax.axis_size(axis)
    if by % size == 0:
        return a
    return lax.ppermute(a, axis, [(i, (i + by) % size) for i in range(size)])


def gather_z(a, early, late, work):
    after, before = [a], [a]
    for step in range(NZ // 2 - 1):
        if step == 2:
            (after[-1], before[-1]), early = lax.optimization_barrier(((after[-1], before[-1]), early))
        after.append(shift(after[-1], "z", -1))
        before.append(shift(before[-1], "z", 1))
    last, late = lax.optimization_barrier(((after[-1], before[-1]), late))
    cut = a.shape[0] // 2
    far = (shift(last[0][:cut], "z", -1), shift(last[1][cut:], "z", 1))
    first = after[:3] + before[1:2]
    first = jnp.concatenate([first[0], first[1], first[3], first[2]], axis=0)
    first = (first, shift(first, "core", 1))
    partial, ws = work(first, early, late)
    far, mine = lax.optimization_barrier((far, partial[0]))
    done = ([mine, partial[1]], ws)
    second = (jnp.concatenate([before[2], last[0], last[1]], axis=0), *far)
    return first, done, (second, tuple(shift(piece, "core", 1) for piece in second))


def by_y_and_z(a, z):
    flat = Z_ORDER[0] + Z_ORDER[1]
    a = a.reshape(NZ, NY, -1, a.shape[-1])
    a = jnp.concatenate([a[flat.index(k)][None] for k in range(NZ)] * 2, axis=0)
    a = lax.dynamic_slice_in_dim(a, NZ - z, NZ, 0)
    return a.transpose(1, 0, 2, 3).reshape(-1, a.shape[-1])


def total(terms):
    return sum(a.astype(F32) for a in terms).astype(BF)


def exchange(a, axes):
    return lax.all_to_all(a, axes, 0, 0, tiled=True)


def to_slices(a):
    return a.reshape(a.shape[0], NX, -1).transpose(1, 0, 2)


def from_slices(a):
    return a.transpose(1, 0, 2).reshape(a.shape[1], -1)


def nt(a, b):
    return lax.dot_general(a, b, (((1,), (1,)), ((), ())), preferred_element_type=F32)


def tn(a, b):
    return lax.dot_general(a, b, (((0,), (0,)), ((), ())), preferred_element_type=F32)


def mm(a, b):
    return jnp.dot(a, b, preferred_element_type=F32)


def three_terms(a):
    hi = a.astype(BF)
    rest = a - hi.astype(F32)
    mid = rest.astype(BF)
    return hi, mid, (rest - mid.astype(F32)).astype(BF)


def dequantize_kernel(x_ref, gm, um, dm, gs, us, ds, w0, w1, w2, w3, keep):
    step = pl.program_id(0)
    hid, groups = gs.shape[1:]
    part = w0.shape[1]
    scales = three_terms(jnp.concatenate([gs[0], us[0], ds[0]], axis=0))
    group = lax.broadcasted_iota(jnp.int32, (groups, part), 0)
    lane_group = lax.broadcasted_iota(jnp.int32, (groups, part), 1) // GROUP
    first = lax.rem(x_ref[0] + step, NX) * (part // GROUP)
    spread = jnp.where(group == lane_group + first, 1.0, 0.0).astype(BF)
    scale = mm(scales[0], spread) + mm(scales[1], spread) + mm(scales[2], spread)
    for p, master in enumerate((gm, um, dm)):
        rows = slice(p * hid, (p + 1) * hid)
        unit = scale[rows]
        ratio = master[0] / unit
        levels = jnp.clip(jnp.floor(ratio + 0.5), -8.0, 7.0)
        weight = (levels * unit).astype(BF)
        for s, w in enumerate((w0, w1, w2, w3)):

            @pl.when(step == s)
            def _(w=w, weight=weight, rows=rows):
                w[rows] = weight

        keep[0, rows] = jnp.where((ratio > -8.5) & (ratio < 7.5), 1.0, 0.0).astype(BF)


def dequantize(x_index, masters, scales):
    _, hid, width = masters[0].shape
    part = width // NX
    grid = pltpu.PrefetchScalarGridSpec(
        num_scalar_prefetch=1,
        grid=(NX,),
        in_specs=[pl.BlockSpec((1, hid, part), lambda i, x: (0, 0, lax.rem(x[0] + i, NX)))] * 3
        + [pl.BlockSpec(scales[0].shape, lambda i, x: (0, 0, 0))] * 3,
        out_specs=[pl.BlockSpec((3 * hid, part), lambda i, x: (0, 0))] * NX
        + [pl.BlockSpec((1, 3 * hid, part), lambda i, x: (i, 0, 0))],
    )
    return pl.pallas_call(
        dequantize_kernel,
        grid_spec=grid,
        out_shape=[jax.ShapeDtypeStruct((3 * hid, part), BF)] * NX
        + [jax.ShapeDtypeStruct((NX, 3 * hid, part), BF)],
        compiler_params=pltpu.CompilerParams(vmem_limit_bytes=VMEM_LIMIT),
        cost_estimate=pl.CostEstimate(
            flops=30 * 3 * hid * width, bytes_accessed=8 * 3 * hid * width, transcendentals=0
        ),
    )(x_index, *masters, *scales)


def finish_kernel(x_ref, r0, r1, r2, r3, keep, og, ou, od):
    hid = og.shape[1]
    part = r0.shape[1]
    for s, r in enumerate((r0, r1, r2, r3)):
        col = pl.multiple_of(lax.rem(x_ref[0] + s, NX) * part, 128)
        for p, out in enumerate((og, ou, od)):
            rows = slice(p * hid, (p + 1) * hid)
            out[0, :, pl.ds(col, part)] = jnp.where(
                keep[s, rows].astype(F32) > 0.0, r[rows].astype(F32), 0.0
            )


def slot_of(found, blocks, toks, s):
    block = lax.broadcasted_iota(jnp.int32, (found.shape[0], 1), 0) // toks
    second = jnp.where(found[:, 2 * s + 1 : 2 * s + 2] > 0.5, block + blocks, -1)
    return jnp.where(found[:, 2 * s : 2 * s + 1] > 0.5, block, second)


def places(slot, slots):
    column = lax.broadcasted_iota(jnp.int32, (slot.shape[0], slots), 1)
    return jnp.where(column == slot, 1.0, 0.0)


def forward_kernel(toks, pick, w0, w1, w2, w3, *refs):
    pieces, (p0, p1, p2, p3, weight, slot) = refs[:-6], refs[-6:]
    ws, outs = (w0, w1, w2, w3), (p0, p1, p2, p3)
    rows = pieces[0]
    if len(pieces) > 1:
        rows = jnp.concatenate([piece[...] for piece in pieces], axis=0)
    part, n, slots = w0.shape[1], rows.shape[0], weight.shape[1]
    gu = 2 * w0.shape[0] // 3
    found = mm(rows[:, 2 * part :], pick[...])
    x, g = rows[:, :part], rows[:, part : 2 * part]
    pre_gu = nt(jnp.concatenate([w[:gu] for w in ws], axis=0), x).astype(BF)
    pre_d = nt(jnp.concatenate([w[gu:] for w in ws], axis=0), g).astype(BF)
    slot[...] = jnp.full(slot.shape, -1, jnp.int32)
    for s, out in enumerate(outs):
        where = slot_of(found, n // toks, toks, s)
        slot[:, s : s + 1] = where
        place = places(where, slots)
        if s == 0:
            weight[...] = jnp.sum(place * found[:, 8:9], axis=0, keepdims=True)
        place = place.astype(BF)
        out[:gu] = mm(pre_gu[s * gu : (s + 1) * gu], place).astype(BF)
        out[gu:] = mm(pre_d[s * gu // 2 : (s + 1) * gu // 2], place).astype(BF)


def weight_grad_kernel(
    experts, s0, s1, s2, s3, da, db, *refs
):
    pieces, (oa, ob, x, g, d_gu, d_h, sems) = refs[:-7], refs[-7:]
    gu = 2 * oa.shape[0] // 3
    slots = da.shape[1] // 4
    n, part = s0.shape[0], oa.shape[1]
    copies = []
    for k, dst in enumerate((x, g)):
        start = 0
        for r in pieces:
            at = pl.ds(start, r.shape[0])
            copies.append(
                pltpu.make_async_copy(
                    r.at[:, pl.ds(k * part, part)], dst.at[at], sems.at[len(copies)]
                )
            )
            start += r.shape[0]
    for copy in copies:
        copy.start()
    for i, slot in enumerate((s0, s1, s2, s3)):
        for j, (s, d) in enumerate(zip(experts, (da, db))):
            spread = nt(
                d[:, i * slots : (i + 1) * slots], places(slot[:, s : s + 1], slots).astype(BF)
            ).astype(BF)
            at = slice(i * n, (i + 1) * n)
            d_gu[j * gu : (j + 1) * gu, at] = spread[:gu]
            d_h[j * gu // 2 : (j + 1) * gu // 2, at] = spread[gu:]
    for copy in copies[: len(pieces)]:
        copy.wait()
    grad = mm(d_gu[...], x[...]).astype(BF)
    oa[:gu] = grad[:gu]
    ob[:gu] = grad[gu:]
    for copy in copies[len(pieces) :]:
        copy.wait()
    grad = mm(d_h[...], g[...]).astype(BF)
    oa[gu:] = grad[: gu // 2]
    ob[gu:] = grad[gu // 2 :]


def weight_grads(experts, slots, groups, delta, part):
    n, rows = slots[0].shape[0], delta[0].shape[0]
    pieces = [piece for group in groups for piece in group]
    gu = 2 * rows // 3
    vmem = pl.BlockSpec(memory_space=pltpu.VMEM)
    return pl.pallas_call(
        functools.partial(weight_grad_kernel, experts),
        out_shape=[jax.ShapeDtypeStruct((rows, part), BF)] * 2,
        in_specs=[vmem] * 6 + [pl.BlockSpec(memory_space=pl.ANY)] * len(pieces),
        out_specs=[vmem] * 2,
        scratch_shapes=[
            pltpu.VMEM((4 * n, part), BF),
            pltpu.VMEM((4 * n, part), BF),
            pltpu.VMEM((2 * gu, 4 * n), BF),
            pltpu.VMEM((gu, 4 * n), BF),
            pltpu.SemaphoreType.DMA((2 * len(pieces),)),
        ],
        compiler_params=pltpu.CompilerParams(vmem_limit_bytes=KERNEL_VMEM),
        cost_estimate=pl.CostEstimate(
            flops=2 * rows * 2 * part * 4 * n,
            bytes_accessed=2 * (8 * n * part + 2 * 2 * rows * part),
            transcendentals=0,
        ),
    )(*slots, *[delta[s] for s in experts], *pieces)


def input_grad(half, slot, ds, ws):
    gu = 2 * ws[0].shape[0] // 3
    slots = ds[0].shape[1] // 2
    spread = jnp.concatenate(
        [
            nt(places(slot[:, s : s + 1], slots).astype(BF), d[:gu, half * slots : (half + 1) * slots])
            for s, d in enumerate(ds)
        ],
        axis=1,
    ).astype(BF)
    return mm(spread, jnp.concatenate([w[:gu] for w in ws], axis=0))


def theirs_kernel(slot, d0, d1, d2, d3, w0, w1, w2, w3, out):
    out[...] = input_grad(1, slot, (d0, d1, d2, d3), (w0, w1, w2, w3)).astype(BF)


def ours_kernel(y_ref, slot, d0, d1, d2, d3, w0, w1, w2, w3, theirs, o0, o1, o2, o3, grad):
    total_grad = input_grad(0, slot, (d0, d1, d2, d3), (w0, w1, w2, w3)) + theirs[...].astype(F32)
    grad[...] = total_grad.astype(BF)
    rows = o0.shape[0]
    for k, out in enumerate((o0, o1, o2, o3)):
        start = pl.multiple_of(lax.rem(y_ref[0] + k, NY) * rows, rows)
        out[...] = grad[pl.ds(start, rows), :]


def local_call(kernel, out_shape, cost, scalars=0, scratch=()):
    vmem = pl.BlockSpec(memory_space=pltpu.VMEM)
    smem = pl.BlockSpec(memory_space=pltpu.SMEM)

    def call(*args):
        return pl.pallas_call(
            kernel,
            out_shape=out_shape,
            in_specs=[smem] * scalars + [vmem] * (len(args) - scalars),
            out_specs=[vmem] * len(out_shape),
            scratch_shapes=list(scratch),
            compiler_params=pltpu.CompilerParams(vmem_limit_bytes=KERNEL_VMEM),
            cost_estimate=pl.CostEstimate(flops=cost[0], bytes_accessed=cost[1], transcendentals=0),
        )(*args)

    return call


def per_device(
    tokens,
    grad_out,
    expert_ids,
    gate_values,
    gate_master,
    gate_scale,
    up_master,
    up_scale,
    down_master,
    down_scale,
):
    x, y, z = (lax.axis_index(name) for name in ("x", "y", "z"))
    experts = NX * lax.axis_size("core")
    expert = x * lax.axis_size("core") + lax.axis_index("core")
    toks, width = tokens.shape
    hid = gate_master.shape[1]
    part = width // NX
    cap = toks // 2
    x_index = x.reshape(1)

    named = expert_ids[:, :, None] == jnp.arange(experts, dtype=jnp.int32)
    factor = jnp.sum(jnp.where(named, gate_values[:, :, None], 0.0), axis=1)
    member = jnp.any(named, axis=1)
    rank = jnp.cumsum(member.astype(jnp.int32), axis=0) - 1
    f_hi = lax.reduce_precision(factor, 8, 7)
    f_mid = lax.reduce_precision(factor - f_hi, 8, 7)
    cols = [f_hi, f_mid, factor - f_hi - f_mid]
    cols += [jnp.where(member & (rank == slot), 1.0, 0.0) for slot in range(cap)]
    cols = jnp.concatenate(cols, axis=1).astype(BF)
    cols = jnp.pad(cols, ((0, 0), (0, 128 - cols.shape[1])))
    payload = jnp.concatenate(
        [to_slices(tokens), to_slices(grad_out), jnp.broadcast_to(cols, (NX,) + cols.shape)], axis=2
    )
    payload = jnp.broadcast_to(payload, (NY,) + payload.shape).reshape(NY * NX, toks, -1)
    own = exchange(payload, ("y", "x")).reshape(NY * NX * toks, -1)
    *w_mine, keep = dequantize(
        x_index, (gate_master, up_master, down_master), (gate_scale, up_scale, down_scale)
    )
    own, w_mine = lax.optimization_barrier((own, w_mine))
    w = [shift(a, "x", s) if s != 2 else a for s, a in enumerate(w_mine)]
    w = lax.optimization_barrier(w)
    n = NY * NZ * NX * toks // 2
    slots = n // toks * cap

    row = jnp.arange(128, dtype=jnp.int32)[:, None]
    col = jnp.arange(128, dtype=jnp.int32)[None, :]
    owner = (col // cap * (experts - 2) + expert) % experts
    pick = (col < cap * NX) & (row == owner + (3 + col % cap) * experts)
    pick |= (col == cap * NX) & (row % experts == expert) & (row < 3 * experts)
    pick = pick.astype(BF)
    row_bytes = 2 * n * own.shape[1]
    w_bytes = 2 * 3 * hid * width
    forward = local_call(
        functools.partial(forward_kernel, toks),
        [jax.ShapeDtypeStruct((3 * hid, slots), BF)] * NX
        + [jax.ShapeDtypeStruct((1, slots), F32), jax.ShapeDtypeStruct((n, 128), jnp.int32)],
        (2 * 3 * hid * width * n, row_bytes + w_bytes),
    )

    def work(rows, early, late):
        ws = (w[0], early[0], late, early[1])
        return [forward(pick, *ws, a) for a in rows], ws

    first, (partial, w), second = gather_z(own, (w[1], w[3]), shift(w[2], "x", 2), work)
    partial = partial + [forward(pick, *w, *a) for a in second]
    groups = [(first[0],), second[0], (first[1],), second[1]]
    partial = [partial[i] for i in (0, 2, 1, 3)]
    weight = jnp.concatenate([p[NX] for p in partial], axis=1)
    pre = [shift(jnp.concatenate([p[s] for p in partial], axis=1), "x", -s) for s in range(NX)]
    slot = [p[NX + 1] for p in partial]
    by_half = [jnp.where(a >= 0, a + i % 2 * slots, -1) for i, a in enumerate(slot)]
    by_half = [by_y_and_z(jnp.concatenate(by_half[i : i + 2], axis=0), z) for i in (0, 2)]

    pre = sum(a.astype(F32) for a in pre)

    gate_pre, up_pre = pre[:hid], pre[hid : 2 * hid]
    delta_hidden = jnp.where(weight > 0.0, pre[2 * hid :] * weight, 0.0)
    sig_gate = jax.nn.sigmoid(gate_pre)
    silu_gate = gate_pre * sig_gate
    hidden = jnp.where(weight > 0.0, silu_gate * up_pre * weight, 0.0)
    delta_up = delta_hidden * silu_gate
    delta_gate = delta_hidden * up_pre * sig_gate * (1.0 + gate_pre * (1.0 - sig_gate))
    delta = jnp.concatenate([delta_gate, delta_up, hidden], axis=0).astype(BF)
    delta = [shift(delta, "x", s) for s in range(NX)]
    half = 2 * n
    theirs = local_call(
        theirs_kernel,
        [jax.ShapeDtypeStruct((half, part), BF)],
        (4 * hid * width * half, row_bytes + w_bytes),
    )(by_half[1], *delta, *w)[0]
    theirs = shift(theirs, "core", 1)
    g_near = weight_grads((1, 3), slot, groups, delta, part)
    theirs, g_near = lax.optimization_barrier((theirs, g_near))
    near = (shift(g_near[0], "x", -1), shift(g_near[1], "x", -3))
    g_own, g_far = weight_grads((0, 2), slot, groups, delta, part)
    unit = NX * toks
    grad_x = local_call(
        ours_kernel,
        [jax.ShapeDtypeStruct((NZ * unit, part), BF)] * NY,
        (4 * hid * width * half, 2 * row_bytes + w_bytes),
        scalars=1,
        scratch=[pltpu.VMEM((half, part), BF)],
    )(y.reshape(1), by_half[0], *delta, *w, theirs)
    grad_x = [shift(g, "y", k) for k, g in enumerate(grad_x)]
    near, g_far = lax.optimization_barrier((near, g_far))
    far = shift(g_far, "x", -2)
    grad_x = total(grad_x).reshape(NZ * NX, toks, part)
    grad_x, far = lax.optimization_barrier((grad_x, far))
    grad_x = exchange(grad_x, ("z", "x"))
    grad_tokens = from_slices(total(list(grad_x.reshape(NZ, NX, toks, part))))

    g_all = (g_own, near[0], far, near[1])
    grads = local_call(
        finish_kernel,
        [jax.ShapeDtypeStruct((1, hid, width), F32)] * 3,
        (3 * 3 * hid * width, 8 * 3 * hid * width),
        scalars=1,
    )(x_index, *g_all, keep)
    return (grad_tokens, *grads)


def solution(mesh):
    mesh = jax.sharding.Mesh(mesh.devices.reshape(NY, NZ, NX, -1), AXES)
    rows = P(AXES, None)
    weights = P(("x", "core"), ("y", "z"), None)
    return jax.shard_map(
        per_device,
        mesh=mesh,
        in_specs=(rows,) * 4 + (weights,) * 6,
        out_specs=(rows,) + (weights,) * 3,
        check_vma=False,
    )
```

```python
import functools

import jax
import jax.numpy as jnp
from jax import lax
from jax.experimental import pallas as pl
from jax.experimental.pallas import tpu as pltpu
from jax.sharding import PartitionSpec as P

NX, NY, NZ = 4, 4, 8
GROUP = 32
Z_ORDER = ((0, 1, 7, 2), (6, 3, 5, 4))
AXES = ("y", "z", "x", "core")
BF = jnp.bfloat16
F32 = jnp.float32
VMEM_LIMIT = 60 * 1024 * 1024
KERNEL_VMEM = 24 * 1024 * 1024


def shift(a, axis, by):
    size = lax.axis_size(axis)
    if by % size == 0:
        return a
    return lax.ppermute(a, axis, [(i, (i + by) % size) for i in range(size)])


def gather_z(a, early, late, work):
    after, before = [a], [a]
    for step in range(NZ // 2 - 1):
        if step == 2:
            (after[-1], before[-1]), early = lax.optimization_barrier(((after[-1], before[-1]), early))
        after.append(shift(after[-1], "z", -1))
        before.append(shift(before[-1], "z", 1))
    last, late = lax.optimization_barrier(((after[-1], before[-1]), late))
    cut = a.shape[0] // 2
    far = (shift(last[0][:cut], "z", -1), shift(last[1][cut:], "z", 1))
    first = after[:3] + before[1:2]
    first = jnp.concatenate([first[0], first[1], first[3], first[2]], axis=0)
    first = (first, shift(first, "core", 1))
    partial, ws = work(first, early, late)
    far, mine = lax.optimization_barrier((far, partial[0]))
    done = ([mine, partial[1]], ws)
    second = (jnp.concatenate([before[2], last[0], last[1]], axis=0), *far)
    return first, done, (second, tuple(shift(piece, "core", 1) for piece in second))


def by_y_and_z(a, z):
    flat = Z_ORDER[0] + Z_ORDER[1]
    a = a.reshape(NZ, NY, -1, a.shape[-1])
    a = jnp.concatenate([a[flat.index(k)][None] for k in range(NZ)] * 2, axis=0)
    a = lax.dynamic_slice_in_dim(a, NZ - z, NZ, 0)
    return a.transpose(1, 0, 2, 3).reshape(-1, a.shape[-1])


def total(terms):
    return sum(a.astype(F32) for a in terms).astype(BF)


def exchange(a, axes):
    return lax.all_to_all(a, axes, 0, 0, tiled=True)


def to_slices(a):
    return a.reshape(a.shape[0], NX, -1).transpose(1, 0, 2)


def from_slices(a):
    return a.transpose(1, 0, 2).reshape(a.shape[1], -1)


def nt(a, b):
    return lax.dot_general(a, b, (((1,), (1,)), ((), ())), preferred_element_type=F32)


def tn(a, b):
    return lax.dot_general(a, b, (((0,), (0,)), ((), ())), preferred_element_type=F32)


def mm(a, b):
    return jnp.dot(a, b, preferred_element_type=F32)


def three_terms(a):
    hi = a.astype(BF)
    rest = a - hi.astype(F32)
    mid = rest.astype(BF)
    return hi, mid, (rest - mid.astype(F32)).astype(BF)


def dequantize_kernel(x_ref, gm, um, dm, gs, us, ds, w0, w1, w2, w3, keep):
    step = pl.program_id(0)
    hid, groups = gs.shape[1:]
    part = w0.shape[1]
    scales = three_terms(jnp.concatenate([gs[0], us[0], ds[0]], axis=0))
    group = lax.broadcasted_iota(jnp.int32, (groups, part), 0)
    lane_group = lax.broadcasted_iota(jnp.int32, (groups, part), 1) // GROUP
    first = lax.rem(x_ref[0] + step, NX) * (part // GROUP)
    spread = jnp.where(group == lane_group + first, 1.0, 0.0).astype(BF)
    scale = mm(scales[0], spread) + mm(scales[1], spread) + mm(scales[2], spread)
    for p, master in enumerate((gm, um, dm)):
        rows = slice(p * hid, (p + 1) * hid)
        unit = scale[rows]
        ratio = master[0] / unit
        levels = jnp.clip(jnp.floor(ratio + 0.5), -8.0, 7.0)
        weight = (levels * unit).astype(BF)
        for s, w in enumerate((w0, w1, w2, w3)):

            @pl.when(step == s)
            def _(w=w, weight=weight, rows=rows):
                w[rows] = weight

        keep[0, rows] = jnp.where((ratio > -8.5) & (ratio < 7.5), 1.0, 0.0).astype(BF)


def dequantize(x_index, masters, scales):
    _, hid, width = masters[0].shape
    part = width // NX
    grid = pltpu.PrefetchScalarGridSpec(
        num_scalar_prefetch=1,
        grid=(NX,),
        in_specs=[pl.BlockSpec((1, hid, part), lambda i, x: (0, 0, lax.rem(x[0] + i, NX)))] * 3
        + [pl.BlockSpec(scales[0].shape, lambda i, x: (0, 0, 0))] * 3,
        out_specs=[pl.BlockSpec((3 * hid, part), lambda i, x: (0, 0))] * NX
        + [pl.BlockSpec((1, 3 * hid, part), lambda i, x: (i, 0, 0))],
    )
    return pl.pallas_call(
        dequantize_kernel,
        grid_spec=grid,
        out_shape=[jax.ShapeDtypeStruct((3 * hid, part), BF)] * NX
        + [jax.ShapeDtypeStruct((NX, 3 * hid, part), BF)],
        compiler_params=pltpu.CompilerParams(vmem_limit_bytes=VMEM_LIMIT),
        cost_estimate=pl.CostEstimate(
            flops=30 * 3 * hid * width, bytes_accessed=8 * 3 * hid * width, transcendentals=0
        ),
    )(x_index, *masters, *scales)


def finish_kernel(x_ref, r0, r1, r2_top, r2_bottom, r3, keep, og, ou, od):
    hid = og.shape[1]
    part = r0.shape[1]
    r2 = jnp.concatenate([r2_top[...], r2_bottom[...]], axis=0)
    for s, r in enumerate((r0, r1, r2, r3)):
        col = pl.multiple_of(lax.rem(x_ref[0] + s, NX) * part, 128)
        for p, out in enumerate((og, ou, od)):
            rows = slice(p * hid, (p + 1) * hid)
            out[0, :, pl.ds(col, part)] = jnp.where(
                keep[s, rows].astype(F32) > 0.0, r[rows].astype(F32), 0.0
            )


def slot_of(found, blocks, toks, s):
    block = lax.broadcasted_iota(jnp.int32, (found.shape[0], 1), 0) // toks
    second = jnp.where(found[:, 2 * s + 1 : 2 * s + 2] > 0.5, block + blocks, -1)
    return jnp.where(found[:, 2 * s : 2 * s + 1] > 0.5, block, second)


def places(slot, slots):
    column = lax.broadcasted_iota(jnp.int32, (slot.shape[0], slots), 1)
    return jnp.where(column == slot, 1.0, 0.0)


def forward_kernel(toks, pick, w0, w1, w2, w3, *refs):
    pieces, (p0, p1, p2, p3, weight, slot) = refs[:-6], refs[-6:]
    ws, outs = (w0, w1, w2, w3), (p0, p1, p2, p3)
    rows = pieces[0]
    if len(pieces) > 1:
        rows = jnp.concatenate([piece[...] for piece in pieces], axis=0)
    part, n, slots = w0.shape[1], rows.shape[0], weight.shape[1]
    gu = 2 * w0.shape[0] // 3
    found = mm(rows[:, 2 * part :], pick[...])
    x, g = rows[:, :part], rows[:, part : 2 * part]
    pre_gu = nt(jnp.concatenate([w[:gu] for w in ws], axis=0), x).astype(BF)
    pre_d = nt(jnp.concatenate([w[gu:] for w in ws], axis=0), g).astype(BF)
    slot[...] = jnp.full(slot.shape, -1, jnp.int32)
    for s, out in enumerate(outs):
        where = slot_of(found, n // toks, toks, s)
        slot[:, s : s + 1] = where
        place = places(where, slots)
        if s == 0:
            weight[...] = jnp.sum(place * found[:, 8:9], axis=0, keepdims=True)
        place = place.astype(BF)
        out[:gu] = mm(pre_gu[s * gu : (s + 1) * gu], place).astype(BF)
        out[gu:] = mm(pre_d[s * gu // 2 : (s + 1) * gu // 2], place).astype(BF)


def weight_grad_kernel(
    experts, s0, s1, s2, s3, da, db, *refs
):
    pieces, (oa, ob, x, g, d_gu, d_h, sems) = refs[:-7], refs[-7:]
    gu = 2 * oa.shape[0] // 3
    slots = da.shape[1] // 4
    n, part = s0.shape[0], oa.shape[1]
    copies = []
    for k, dst in enumerate((x, g)):
        start = 0
        for r in pieces:
            at = pl.ds(start, r.shape[0])
            copies.append(
                pltpu.make_async_copy(
                    r.at[:, pl.ds(k * part, part)], dst.at[at], sems.at[len(copies)]
                )
            )
            start += r.shape[0]
    for copy in copies:
        copy.start()
    for i, slot in enumerate((s0, s1, s2, s3)):
        for j, (s, d) in enumerate(zip(experts, (da, db))):
            spread = nt(
                d[:, i * slots : (i + 1) * slots], places(slot[:, s : s + 1], slots).astype(BF)
            ).astype(BF)
            at = slice(i * n, (i + 1) * n)
            d_gu[j * gu : (j + 1) * gu, at] = spread[:gu]
            d_h[j * gu // 2 : (j + 1) * gu // 2, at] = spread[gu:]
    for copy in copies[: len(pieces)]:
        copy.wait()
    grad = mm(d_gu[...], x[...]).astype(BF)
    oa[:gu] = grad[:gu]
    ob[:gu] = grad[gu:]
    for copy in copies[len(pieces) :]:
        copy.wait()
    grad = mm(d_h[...], g[...]).astype(BF)
    oa[gu:] = grad[: gu // 2]
    ob[gu:] = grad[gu // 2 :]


def weight_grads(experts, slots, groups, delta, part):
    n, rows = slots[0].shape[0], delta[0].shape[0]
    pieces = [piece for group in groups for piece in group]
    gu = 2 * rows // 3
    vmem = pl.BlockSpec(memory_space=pltpu.VMEM)
    return pl.pallas_call(
        functools.partial(weight_grad_kernel, experts),
        out_shape=[jax.ShapeDtypeStruct((rows, part), BF)] * 2,
        in_specs=[vmem] * 6 + [pl.BlockSpec(memory_space=pl.ANY)] * len(pieces),
        out_specs=[vmem] * 2,
        scratch_shapes=[
            pltpu.VMEM((4 * n, part), BF),
            pltpu.VMEM((4 * n, part), BF),
            pltpu.VMEM((2 * gu, 4 * n), BF),
            pltpu.VMEM((gu, 4 * n), BF),
            pltpu.SemaphoreType.DMA((2 * len(pieces),)),
        ],
        compiler_params=pltpu.CompilerParams(vmem_limit_bytes=KERNEL_VMEM),
        cost_estimate=pl.CostEstimate(
            flops=2 * rows * 2 * part * 4 * n,
            bytes_accessed=2 * (8 * n * part + 2 * 2 * rows * part),
            transcendentals=0,
        ),
    )(*slots, *[delta[s] for s in experts], *pieces)


def input_grad(half, slot, ds, ws):
    gu = 2 * ws[0].shape[0] // 3
    slots = ds[0].shape[1] // 2
    spread = jnp.concatenate(
        [
            nt(places(slot[:, s : s + 1], slots).astype(BF), d[:gu, half * slots : (half + 1) * slots])
            for s, d in enumerate(ds)
        ],
        axis=1,
    ).astype(BF)
    return mm(spread, jnp.concatenate([w[:gu] for w in ws], axis=0))


def theirs_kernel(slot, d0, d1, d2, d3, w0, w1, w2, w3, out):
    out[...] = input_grad(1, slot, (d0, d1, d2, d3), (w0, w1, w2, w3)).astype(BF)


def ours_kernel(y_ref, slot, d0, d1, d2, d3, w0, w1, w2, w3, theirs, o0, o1, o2, o3, grad):
    total_grad = input_grad(0, slot, (d0, d1, d2, d3), (w0, w1, w2, w3)) + theirs[...].astype(F32)
    grad[...] = total_grad.astype(BF)
    rows = o0.shape[0]
    for k, out in enumerate((o0, o1, o2, o3)):
        start = pl.multiple_of(lax.rem(y_ref[0] + k, NY) * rows, rows)
        out[...] = grad[pl.ds(start, rows), :]


def local_call(kernel, out_shape, cost, scalars=0, scratch=()):
    vmem = pl.BlockSpec(memory_space=pltpu.VMEM)
    smem = pl.BlockSpec(memory_space=pltpu.SMEM)

    def call(*args):
        return pl.pallas_call(
            kernel,
            out_shape=out_shape,
            in_specs=[smem] * scalars + [vmem] * (len(args) - scalars),
            out_specs=[vmem] * len(out_shape),
            scratch_shapes=list(scratch),
            compiler_params=pltpu.CompilerParams(vmem_limit_bytes=KERNEL_VMEM),
            cost_estimate=pl.CostEstimate(flops=cost[0], bytes_accessed=cost[1], transcendentals=0),
        )(*args)

    return call


def per_device(
    tokens,
    grad_out,
    expert_ids,
    gate_values,
    gate_master,
    gate_scale,
    up_master,
    up_scale,
    down_master,
    down_scale,
):
    x, y, z = (lax.axis_index(name) for name in ("x", "y", "z"))
    experts = NX * lax.axis_size("core")
    expert = x * lax.axis_size("core") + lax.axis_index("core")
    toks, width = tokens.shape
    hid = gate_master.shape[1]
    part = width // NX
    cap = toks // 2
    x_index = x.reshape(1)

    named = expert_ids[:, :, None] == jnp.arange(experts, dtype=jnp.int32)
    factor = jnp.sum(jnp.where(named, gate_values[:, :, None], 0.0), axis=1)
    member = jnp.any(named, axis=1)
    rank = jnp.cumsum(member.astype(jnp.int32), axis=0) - 1
    f_hi = lax.reduce_precision(factor, 8, 7)
    f_mid = lax.reduce_precision(factor - f_hi, 8, 7)
    cols = [f_hi, f_mid, factor - f_hi - f_mid]
    cols += [jnp.where(member & (rank == slot), 1.0, 0.0) for slot in range(cap)]
    cols = jnp.concatenate(cols, axis=1).astype(BF)
    cols = jnp.pad(cols, ((0, 0), (0, 128 - cols.shape[1])))
    payload = jnp.concatenate(
        [to_slices(tokens), to_slices(grad_out), jnp.broadcast_to(cols, (NX,) + cols.shape)], axis=2
    )
    payload = jnp.broadcast_to(payload, (NY,) + payload.shape).reshape(NY * NX, toks, -1)
    own = exchange(payload, ("y", "x")).reshape(NY * NX * toks, -1)
    *w_mine, keep = dequantize(
        x_index, (gate_master, up_master, down_master), (gate_scale, up_scale, down_scale)
    )
    own, w_mine = lax.optimization_barrier((own, w_mine))
    w = [shift(a, "x", s) if s != 2 else a for s, a in enumerate(w_mine)]
    w = lax.optimization_barrier(w)
    n = NY * NZ * NX * toks // 2
    slots = n // toks * cap

    row = jnp.arange(128, dtype=jnp.int32)[:, None]
    col = jnp.arange(128, dtype=jnp.int32)[None, :]
    owner = (col // cap * (experts - 2) + expert) % experts
    pick = (col < cap * NX) & (row == owner + (3 + col % cap) * experts)
    pick |= (col == cap * NX) & (row % experts == expert) & (row < 3 * experts)
    pick = pick.astype(BF)
    row_bytes = 2 * n * own.shape[1]
    w_bytes = 2 * 3 * hid * width
    forward = local_call(
        functools.partial(forward_kernel, toks),
        [jax.ShapeDtypeStruct((3 * hid, slots), BF)] * NX
        + [jax.ShapeDtypeStruct((1, slots), F32), jax.ShapeDtypeStruct((n, 128), jnp.int32)],
        (2 * 3 * hid * width * n, row_bytes + w_bytes),
    )

    def work(rows, early, late):
        ws = (w[0], early[0], late, early[1])
        return [forward(pick, *ws, a) for a in rows], ws

    first, (partial, w), second = gather_z(own, (w[1], w[3]), shift(w[2], "x", 2), work)
    partial = partial + [forward(pick, *w, *a) for a in second]
    groups = [(first[0],), second[0], (first[1],), second[1]]
    partial = [partial[i] for i in (0, 2, 1, 3)]
    weight = jnp.concatenate([p[NX] for p in partial], axis=1)
    pre = [shift(jnp.concatenate([p[s] for p in partial], axis=1), "x", -s) for s in range(NX)]
    slot = [p[NX + 1] for p in partial]
    by_half = [jnp.where(a >= 0, a + i % 2 * slots, -1) for i, a in enumerate(slot)]
    by_half = [by_y_and_z(jnp.concatenate(by_half[i : i + 2], axis=0), z) for i in (0, 2)]

    pre = sum(a.astype(F32) for a in pre)

    gate_pre, up_pre = pre[:hid], pre[hid : 2 * hid]
    delta_hidden = jnp.where(weight > 0.0, pre[2 * hid :] * weight, 0.0)
    sig_gate = jax.nn.sigmoid(gate_pre)
    silu_gate = gate_pre * sig_gate
    hidden = jnp.where(weight > 0.0, silu_gate * up_pre * weight, 0.0)
    delta_up = delta_hidden * silu_gate
    delta_gate = delta_hidden * up_pre * sig_gate * (1.0 + gate_pre * (1.0 - sig_gate))
    delta = jnp.concatenate([delta_gate, delta_up, hidden], axis=0).astype(BF)
    delta = [shift(delta, "x", s) for s in range(NX)]
    half = 2 * n
    theirs = local_call(
        theirs_kernel,
        [jax.ShapeDtypeStruct((half, part), BF)],
        (4 * hid * width * half, row_bytes + w_bytes),
    )(by_half[1], *delta, *w)[0]
    theirs = shift(theirs, "core", 1)
    g_near = weight_grads((1, 3), slot, groups, delta, part)
    theirs, g_near = lax.optimization_barrier((theirs, g_near))
    near = (shift(g_near[0], "x", -1), shift(g_near[1], "x", -3))
    g_own, g_far = weight_grads((0, 2), slot, groups, delta, part)
    unit = NX * toks
    grad_x = local_call(
        ours_kernel,
        [jax.ShapeDtypeStruct((NZ * unit, part), BF)] * NY,
        (4 * hid * width * half, 2 * row_bytes + w_bytes),
        scalars=1,
        scratch=[pltpu.VMEM((half, part), BF)],
    )(y.reshape(1), by_half[0], *delta, *w, theirs)
    grad_x = [shift(g, "y", k) for k, g in enumerate(grad_x)]
    near, g_far = lax.optimization_barrier((near, g_far))
    top, bottom = g_far[: 2 * hid], g_far[2 * hid :]
    grad_x = total(grad_x).reshape(NZ * NX, toks, part)
    grad_x, top, bottom = lax.optimization_barrier((grad_x, shift(top, "x", -2), bottom))
    bottom = shift(bottom, "x", -2)
    grad_x = exchange(grad_x, ("z", "x"))
    grad_tokens = from_slices(total(list(grad_x.reshape(NZ, NX, toks, part))))

    g_all = (g_own, near[0], top, bottom, near[1])
    grads = local_call(
        finish_kernel,
        [jax.ShapeDtypeStruct((1, hid, width), F32)] * 3,
        (3 * 3 * hid * width, 8 * 3 * hid * width),
        scalars=1,
    )(x_index, *g_all, keep)
    return (grad_tokens, *grads)


def solution(mesh):
    mesh = jax.sharding.Mesh(mesh.devices.reshape(NY, NZ, NX, -1), AXES)
    rows = P(AXES, None)
    weights = P(("x", "core"), ("y", "z"), None)
    return jax.shard_map(
        per_device,
        mesh=mesh,
        in_specs=(rows,) * 4 + (weights,) * 6,
        out_specs=(rows,) + (weights,) * 3,
        check_vma=False,
    )
```
